1024 devices in a mesh: seq: 16 (over y_hi, x), dp: 64 (over z, y_lo, core).
Axes of the slice: x: 8, y: 8 (y_hi: 2, y_lo: 4; y = y_hi * 4 + y_lo), z: 8, core: 2. Of those that a mesh axis runs over, the one named last changes fastest.
Arguments:
- attn_out: bfloat16 [131072, 3072], P('dp', 'seq'), may hold values from -6 to 6
- cotangent: bfloat16 [131072, 3072], P(('seq', 'dp')), may hold values from -0.0625 to 0.0625
- gate: float32 [64, 3072], P('dp'), may hold values from -4 to 4
- weight: float32 [3072, 3072], P('dp', 'seq'), may hold values from -1.5 to 1.5
- exp_avg: float32 [3072, 3072], P('dp', 'seq'), may hold values from -6 to 6
- exp_avg_sq: float32 [3072, 3072], P('dp', 'seq'), may hold values from 0.25 to 4
- left_stats: float32 [3072, 768], P('dp', 'seq'), as said below
- right_stats: float32 [12288, 3072], P('dp', 'seq')
- left_basis: float32 [3072, 768], P('dp', 'seq'), may hold values from -0.875 to 0.875
- right_basis: float32 [12288, 3072], P('dp', 'seq'), may hold values from -0.4375 to 0.4375
Outputs:
- update: float32 [3072, 3072], P('dp', 'seq')
- new_weight: float32 [3072, 3072], P('dp', 'seq')
- new_exp_avg: float32 [3072, 3072], P('dp', 'seq')
- new_exp_avg_sq: float32 [3072, 3072], P('dp', 'seq')
- new_left_stats: float32 [3072, 768], P('dp', 'seq')
- new_right_stats: float32 [12288, 3072], P('dp', 'seq')
The draws below stay inside these ranges and needn't reach their ends.
Inputs may be any that keep to these rules, and one draw needn't show every extreme that they name: Every 48 x 48 block of left_stats and 192 x 192 block of right_stats is symmetric.
All inputs are finite; a program needn't handle non-finite values.
Results may differ from the reference program's by a relative error of at most 0.0003.
Values may be sent and summed in bfloat16 or wider, within the bound.
No kernel may reach another device: no remote copies, remote signals or barrier semaphores. Data moves between devices by JAX's collectives and lax.ppermute only.
A program may use at most 64 MiB of HBM per device.

```python
import math
from functools import partial
import jax
import jax.numpy as jnp
from jax import lax

D = 3072
GROUP_TOK = 2048
HD = 3072
TOK_DEV = 128
TOKENS = 131072
LB = 48
HB = 192
N_SEQ = 16
N_DP = 64


def symmetric(key, blocks_down, side, blocks_across):
    drawn = jax.random.normal(key, (blocks_down, side, blocks_across, side), jnp.float32)
    mirrored = 0.5 * (drawn + drawn.transpose(0, 3, 2, 1))
    diagonal = 3.0 * jnp.eye(side, dtype=jnp.float32)[None, :, None, :]
    return (mirrored + diagonal).reshape(blocks_down * side, blocks_across * side)


def draw_left_stats(key, part):
    key = jax.random.fold_in(key, 1)
    return symmetric(key, D // LB, LB, HD // HB)


def draw_right_stats(key, part):
    key = jax.random.fold_in(key, 2)
    return symmetric(key, D // LB, HB, HD // HB)


def with_spikes(values, key, source, target, parts, factor):
    owner, partner = [(jnp.arange(values.shape[position]) // (values.shape[position] // parts)).reshape([-1 if axis == position else 1 for axis in range(values.ndim)]) for position in (source, target)]
    chosen = jax.random.permutation(key, parts)[partner]
    strong = (owner == chosen) | (owner == (partner + parts // 2) % parts)
    return jnp.where(strong, factor * values, values)


def level_of(rng, extent, pieces, smallest, top_value):
    factor_of, own = 1.0, jax.random.fold_in(rng, 6)
    for axis_at, parts in pieces:
        steps = jnp.exp(jax.random.uniform(jax.random.fold_in(own, axis_at), (parts,), jnp.float32, smallest / len(pieces), top_value / len(pieces)))
        factor_of = factor_of * jnp.repeat(steps, extent[axis_at] // parts).reshape([-1 if axis == axis_at else 1 for axis in range(len(extent))])
    return factor_of


def scatter_about(key, extent, scale, bound, cuts=(), kind=jnp.bfloat16):
    values = scale * jax.random.normal(key, extent, jnp.float32)
    if cuts:
        values = values * level_of(key, extent, cuts, -0.22, 0.18)
    return jnp.clip(values, -bound, bound).astype(kind)


def noise_with(own_key, shape, scale, most, split, heavy, held_as=jnp.bfloat16):
    values = scale * jax.random.normal(own_key, shape, jnp.float32)
    if split:
        values = values * level_of(own_key, shape, split, -0.22, 0.18)
    return jnp.clip(with_spikes(values, jax.random.fold_in(own_key, 3), *heavy), -most, most).astype(held_as)


def setup_inputs(seed: int = 0) -> dict:
    arg_keys = jax.random.split(jax.random.key(seed), 11)
    attn_out = scatter_about(arg_keys[0], (TOKENS, HD), 1.0, 6.0, ((0, 64), (1, 16)))
    cotangent = noise_with(arg_keys[1], (TOKENS, D), (1.0 / (GROUP_TOK * N_DP) ** 0.5), 0.0625, ((0, 1024),), (0, 1, 1024, 6.0))
    gate = scatter_about(arg_keys[2], (N_DP, D), 1.0, 4.0, ((0, 64),), jnp.float32)
    weight = scatter_about(arg_keys[3], (D, HD), 0.25, 1.5, ((0, 64), (1, 16)), jnp.float32)
    exp_avg = scatter_about(arg_keys[4], (D, HD), 1.0, 6.0, ((0, 64), (1, 16)), jnp.float32)
    exp_avg_sq = jnp.clip(jnp.exp(math.log(4.0) - 2.7725887 * jax.random.uniform(arg_keys[5], (D, HD), jnp.float32) ** level_of(arg_keys[5], (D, HD), ((0, 64), (1, 16)), -0.2, 0.2)), 0.25, 4.0)
    left_stats = draw_left_stats(jax.random.fold_in(arg_keys[10], 71), 0)
    right_stats = draw_right_stats(jax.random.fold_in(arg_keys[10], 71), 0)
    left_basis = scatter_about(arg_keys[8], (D, N_SEQ * LB), LB ** -0.5, 0.875, ((0, 64), (1, 16)), jnp.float32)
    right_basis = scatter_about(arg_keys[9], (N_DP * HB, HD), HB ** -0.5, 0.4375, ((0, 64), (1, 16)), jnp.float32)
    return {"attn_out": attn_out, "cotangent": cotangent, "gate": gate, "weight": weight, "exp_avg": exp_avg, "exp_avg_sq": exp_avg_sq, "left_stats": left_stats, "right_stats": right_stats, "left_basis": left_basis, "right_basis": right_basis}


beta_one = 0.9
beta_two = 0.95
epsilon = 1e-08
learn_rate = 0.02
decay_rate = 0.1

def to_blocks(matrix, height, width):
    return matrix.reshape(N_DP, height, N_SEQ, width).transpose(0, 2, 1, 3)

def from_blocks(blocks_in):
    shaped = blocks_in.transpose(0, 2, 1, 3)
    return shaped.reshape(shaped.shape[0] * shaped.shape[1], shaped.shape[2] * shaped.shape[3])

def reference(attn_out, cotangent, gate, weight, exp_avg, exp_avg_sq, left_stats, right_stats, left_basis, right_basis):
    outs_grouped = attn_out.reshape(N_DP, GROUP_TOK, HD)
    cots_grouped = cotangent.reshape(N_SEQ, N_DP, TOK_DEV, D).transpose(1, 0, 2, 3).reshape(N_DP, GROUP_TOK, D)

    def add_clip(running, inputs):
        clip_out, clip_cot, clip_gate = inputs
        term = lax.dot_general(clip_cot, clip_out, (((0,), (0,)), ((), ())), preferred_element_type=jnp.float32)
        return (running + clip_gate[:, None] * term, None)
    gradient, unused = lax.scan(add_clip, jnp.zeros((D, HD), jnp.float32), (outs_grouped, cots_grouped, gate))
    einsum_hi = partial(jnp.einsum, precision=lax.Precision.HIGHEST)
    grad_b = to_blocks(gradient, LB, HB)
    left_q = to_blocks(left_basis, LB, LB)
    right_q = to_blocks(right_basis, HB, HB)
    left_new = beta_two * to_blocks(left_stats, LB, LB) + (1.0 - beta_two) * einsum_hi('abik,abjk->abij', grad_b, grad_b)
    right_new = beta_two * to_blocks(right_stats, HB, HB) + (1.0 - beta_two) * einsum_hi('abki,abkj->abij', grad_b, grad_b)
    moment = beta_one * to_blocks(exp_avg, LB, HB) + (1.0 - beta_one) * grad_b

    def rotate_in(matrix):
        partial_rot = einsum_hi('abki,abkj->abij', left_q, matrix)
        return einsum_hi('abik,abkj->abij', partial_rot, right_q)
    rotated = rotate_in(grad_b)
    second = beta_two * to_blocks(exp_avg_sq, LB, HB) + (1.0 - beta_two) * rotated * rotated
    direction = rotate_in(moment) / (jnp.sqrt(second) + epsilon)
    partial_back = einsum_hi('abik,abkj->abij', left_q, direction)
    update = einsum_hi('abik,abjk->abij', partial_back, right_q)
    new_weight = to_blocks(weight, LB, HB) * (1.0 - learn_rate * decay_rate) - learn_rate * update
    return (from_blocks(update), from_blocks(new_weight), from_blocks(moment), from_blocks(second), from_blocks(left_new), from_blocks(right_new))
```

```python
import jax
import jax.numpy as jnp
from jax import lax
from jax.sharding import Mesh, PartitionSpec as P

beta_one = 0.9
beta_two = 0.95
epsilon = 1e-08
learn_rate = 0.02
decay_rate = 0.1

D = 3072
LB = 48
HB = 192
NX = 8
NZ = 8
NY = 4
TOK = 1024
PIECES = 4
Z_PIECE = NZ // PIECES
WIDTH = D // PIECES
ROW = ("z", "yl", "c")
COL = ("yh", "x")


def hi_dot(left_mat, right_mat):
    return jnp.dot(left_mat, right_mat, precision=lax.Precision.HIGHEST)


def own_half(attn_out):
    yh = lax.axis_index("yh")
    keep = lax.dynamic_slice_in_dim(attn_out, yh * TOK, TOK, 0)
    send = lax.dynamic_slice_in_dim(attn_out, (1 - yh) * TOK, TOK, 0)
    came = lax.ppermute(send, "yh", [(0, 1), (1, 0)])
    first = yh == 0
    return jnp.where(first, keep, came), jnp.where(first, came, keep)


def piece_sum(gathered, halves, gate_rows):
    core = lax.axis_index("c")
    parts = []
    for half in halves:
        product = lax.dot_general(
            gathered, half, (((0,), (0,)), ((), ())), preferred_element_type=jnp.float32
        )
        product = gate_rows[:, None] * product
        parts.append(product.reshape(Z_PIECE, NY, 2, LB, HB).transpose(2, 1, 0, 3, 4))
    both = jnp.stack(parts, axis=1)
    mine = lax.dynamic_index_in_dim(both, core, 0, keepdims=False)
    other = lax.dynamic_index_in_dim(both, 1 - core, 0, keepdims=False)
    paired = mine + lax.ppermute(other, "c", [(0, 1), (1, 0)])
    paired = paired.reshape(2 * NY, Z_PIECE, LB, HB)
    return jnp.sum(lax.all_to_all(paired, ("yh", "yl"), 0, 0), axis=0)


def local(
    attn_out,
    cotangent,
    gate,
    weight,
    exp_avg,
    exp_avg_sq,
    left_stats,
    right_stats,
    left_basis,
    right_basis,
):
    gate_row = gate[0]
    spans = [slice(at * WIDTH, (at + 1) * WIDTH) for at in range(PIECES)]
    gathered = [lax.all_gather(cotangent[:, span], "x", axis=0, tiled=True) for span in spans]
    halves = own_half(attn_out)
    by_z = [piece_sum(got, halves, gate_row[span]) for got, span in zip(gathered, spans)]
    by_z = jnp.concatenate(by_z, axis=0)
    gradient = jnp.sum(lax.all_to_all(by_z, "z", 0, 0), axis=0)

    left_new = beta_two * left_stats + (1.0 - beta_two) * hi_dot(gradient, gradient.T)
    right_new = beta_two * right_stats + (1.0 - beta_two) * hi_dot(gradient.T, gradient)
    moment = beta_one * exp_avg + (1.0 - beta_one) * gradient

    def rotate_in(matrix):
        return hi_dot(hi_dot(left_basis.T, matrix), right_basis)

    rotated = rotate_in(gradient)
    second = beta_two * exp_avg_sq + (1.0 - beta_two) * rotated * rotated
    direction = rotate_in(moment) / (jnp.sqrt(second) + epsilon)
    update = hi_dot(hi_dot(left_basis, direction), right_basis.T)
    new_weight = weight * (1.0 - learn_rate * decay_rate) - learn_rate * update
    return (update, new_weight, moment, second, left_new, right_new)


def solution(mesh):
    fine = Mesh(mesh.devices.reshape(2, NX, NZ, NY, 2), ("yh", "x", "z", "yl", "c"))
    block = P(ROW, COL)
    in_specs = (block, P(COL + ROW, None), P(ROW, None)) + (block,) * 7
    return jax.shard_map(
        local, mesh=fine, in_specs=in_specs, out_specs=(block,) * 6, check_vma=False
    )
```

```python
import functools

import jax
import jax.numpy as jnp
from jax import lax
from jax.experimental import pallas as pl
from jax.experimental.pallas import tpu as pltpu
from jax.sharding import Mesh, PartitionSpec as P

beta_one = 0.9
beta_two = 0.95
epsilon = 1e-08
learn_rate = 0.02
decay_rate = 0.1

D = 3072
LB = 48
HB = 192
NX = 8
NZ = 8
NY = 4
CHUNK = 128
TOK = NX * CHUNK
FEAT = 2 * HB
GROUP = D // NZ
HALF = LB // 2
PACK = (LB * HB) // 128
PIECES = (2, 2, 2, 2)
ROW = ("z", "yl", "c")
COL = ("yh", "x")
Y = ("yh", "yl")
SWAP = [(0, 1), (1, 0)]
RING = [(2 * x + c, 2 * ((x + (1, -1)[c]) % NX) + c) for x in range(NX) for c in range(2)]


def product_kernel(
    place, att_own, att_oth, first, hop_one, hop_two, hop_three, last, gate_own, gate_oth, keep, send
):
    def term(att, at, block):
        columns = pl.ds(pl.multiple_of(place[1 + at] * CHUNK, CHUNK), CHUNK)
        return jnp.dot(att[:, columns], block, preferred_element_type=jnp.float32)

    own = term(att_own, 0, first[0]) + term(att_own, 4, last[...])
    oth = jnp.zeros_like(own)
    for at, hop in ((1, hop_one), (2, hop_two), (3, hop_three)):
        own += term(att_own, at, hop[0])
        oth += term(att_oth, at, hop[1])
    total = gate_own[...] * own + gate_oth[...] * oth
    packed = []
    for yh in range(2):
        at = yh * HB
        rest = total[at + 128 : at + HB]
        moved = pltpu.roll(rest, GROUP - HALF, 1)
        packed.append((total[at : at + 128].T, jnp.concatenate([rest, moved], axis=0).T))

    def store(ref, core):
        for yh in range(2):
            for yl in range(NY):
                at = (2 * yl + core) * LB
                ref[NY * yh + yl, 0, :LB] = packed[yh][0][at : at + LB]
                ref[NY * yh + yl, 0, LB:] = packed[yh][1][at : at + HALF]

    for core in range(2):

        @pl.when(place[0] == core)
        def _():
            store(keep, core)
            store(send, 1 - core)


def product(place, att_own, att_oth, blocks, gate_own, gate_oth):
    count = gate_own.shape[1] // GROUP
    whole = pl.BlockSpec((FEAT, TOK), lambda z: (0, 0))
    pair = pl.BlockSpec((2, CHUNK, GROUP), lambda z: (0, 0, z))
    row = pl.BlockSpec((1, GROUP), lambda z: (0, z))
    out = pl.BlockSpec((2 * NY, 1, PACK, 128), lambda z: (0, z, 0, 0))
    shape = jax.ShapeDtypeStruct((2 * NY, count, PACK, 128), jnp.float32)
    flops = 2 * 8 * CHUNK * FEAT * GROUP * count
    return pl.pallas_call(
        product_kernel,
        grid=(count,),
        in_specs=[pl.BlockSpec(memory_space=pltpu.SMEM), whole, whole, pair, pair, pair, pair]
        + [pl.BlockSpec((CHUNK, GROUP), lambda z: (0, z)), row, row],
        out_specs=[out, out],
        out_shape=[shape, shape],
        cost_estimate=pl.CostEstimate(flops=flops, bytes_accessed=6 << 20, transcendentals=0),
        compiler_params=pltpu.CompilerParams(vmem_limit_bytes=24 << 20),
        name="product",
    )(place, att_own, att_oth, *blocks, gate_own, gate_oth)


def update_kernel(
    parts,
    weight,
    exp_avg,
    exp_avg_sq,
    left_stats,
    right_stats,
    left_basis,
    right_basis,
    update,
    new_weight,
    moment_out,
    second_out,
    left_new,
    right_new,
):
    def dot(left, right, dims):
        return lax.dot_general(
            left,
            right,
            (dims, ((), ())),
            precision=lax.Precision.HIGHEST,
            preferred_element_type=jnp.float32,
        )

    plain, first, last = ((1,), (0,)), ((0,), (0,)), ((1,), (1,))
    packed = jnp.sum(parts[...], axis=0)
    rest = jnp.concatenate([packed[LB:, : HB - 128], packed[LB:, HB - 128 :]], axis=0)
    gradient = jnp.concatenate([packed[:LB], rest], axis=1)
    left_q, right_q = left_basis[...], right_basis[...]
    moment = beta_one * exp_avg[...] + (1.0 - beta_one) * gradient
    moment_out[...] = moment
    rotated = dot(dot(left_q, gradient, first), right_q, plain)
    second = beta_two * exp_avg_sq[...] + (1.0 - beta_two) * rotated * rotated
    second_out[...] = second
    turned = dot(dot(left_q, moment, first), right_q, plain)
    direction = turned / (jnp.sqrt(second) + epsilon)
    step = dot(dot(left_q, direction, plain), right_q, last)
    update[...] = step
    new_weight[...] = weight[...] * (1.0 - learn_rate * decay_rate) - learn_rate * step
    left_new[...] = beta_two * left_stats[...] + (1.0 - beta_two) * dot(gradient, gradient, last)
    right_new[...] = beta_two * right_stats[...] + (1.0 - beta_two) * dot(gradient, gradient, first)


def local(
    attn_out,
    cotangent,
    gate,
    weight,
    exp_avg,
    exp_avg_sq,
    left_stats,
    right_stats,
    left_basis,
    right_basis,
):
    yh, x, core = lax.axis_index("yh"), lax.axis_index("x"), lax.axis_index("c")
    step = 1 - 2 * core
    place = jnp.stack([core] + [lax.rem(x - step * hop + NX, NX) for hop in range(5)])

    spans, at = [], 0
    for count in PIECES:
        spans.append(slice(at, at + count * GROUP))
        at += count * GROUP
    rings = []
    for span in spans:
        own = cotangent[:, span]
        blocks = [jnp.stack([own, lax.ppermute(own, "c", SWAP)])]
        for _ in range(3):
            blocks.append(lax.ppermute(blocks[-1], ("x", "c"), RING))
        blocks.append(lax.ppermute(blocks[-1][0], ("x", "c"), RING))
        rings.append(blocks)

    features = attn_out.T
    kept = lax.dynamic_slice_in_dim(features, yh * TOK, TOK, 1)
    came = lax.ppermute(
        lax.dynamic_slice_in_dim(features, (1 - yh) * TOK, TOK, 1), "yh", SWAP
    )
    att_own = jnp.concatenate(
        [jnp.where(yh == 0, kept, came), jnp.where(yh == 0, came, kept)], axis=0
    )
    att_oth = lax.ppermute(att_own, "c", SWAP)
    gate_oth = lax.ppermute(gate, "c", SWAP)

    by_z = []
    for span, blocks in zip(spans, rings):
        keep, send = product(
            place, att_own, att_oth, blocks, gate[:, span], gate_oth[:, span]
        )
        paired = keep + lax.ppermute(send, "c", SWAP)
        by_z.append(jnp.sum(lax.all_to_all(paired, Y, 0, 0), axis=0))
    parts = lax.all_to_all(jnp.concatenate(by_z, axis=0), "z", 0, 0)

    block = jax.ShapeDtypeStruct((LB, HB), jnp.float32)
    return pl.pallas_call(
        update_kernel,
        out_shape=[block] * 4
        + [
            jax.ShapeDtypeStruct((LB, LB), jnp.float32),
            jax.ShapeDtypeStruct((HB, HB), jnp.float32),
        ],
        name="update",
    )(parts, weight, exp_avg, exp_avg_sq, left_stats, right_stats, left_basis, right_basis)


def solution(mesh):
    fine = Mesh(mesh.devices.reshape(2, NX, NZ, NY, 2), ("yh", "x", "z", "yl", "c"))
    block = P(ROW, COL)
    in_specs = (block, P(COL + ROW, None), P(ROW, None)) + (block,) * 7
    return jax.shard_map(
        local, mesh=fine, in_specs=in_specs, out_specs=(block,) * 6, check_vma=False
    )
```

```python
import functools

import jax
import jax.numpy as jnp
from jax import lax
from jax.experimental import pallas as pl
from jax.experimental.pallas import tpu as pltpu
from jax.sharding import Mesh, PartitionSpec as P

beta_one = 0.9
beta_two = 0.95
epsilon = 1e-08
learn_rate = 0.02
decay_rate = 0.1

D = 3072
LB = 48
HB = 192
NX = 8
NZH = 4
NY = 4
CHUNK = 128
TOK = NX * CHUNK
FEAT = 2 * HB
GROUP = D // 8
HALF = LB // 2
PACK = (LB * HB) // 128
PIECES = ((0, 1), (2, 3))
ROW = ("zh", "zl", "yl", "c")
COL = ("yh", "x")
Y = ("yh", "yl")
SWAP = [(0, 1), (1, 0)]


def at_ring(x, zl, c):
    return (x % NX) * 4 + 2 * zl + c


def ring(other_z, other_core):
    pairs = []
    for x in range(NX):
        for zl in range(2):
            for c in range(2):
                to_z, to_c = zl ^ other_z, c ^ other_core
                pairs.append((at_ring(x, zl, c), at_ring(x + 1 - 2 * to_c, to_z, to_c)))
    return pairs


def hop(block, other_z=0, other_core=0):
    return lax.ppermute(block, ("x", "zl", "c"), ring(other_z, other_core))


def split_kernel(place, cotangent, mine_one, mine_two, other_one, other_two, other_all):
    for zh in range(NZH):
        span = slice((zh % 2) * GROUP, (zh % 2 + 1) * GROUP)
        for parity, ref in ((place[6], (mine_one, mine_two)), (1 - place[6], (other_one, other_two))):
            start = pl.multiple_of((2 * zh + parity) * GROUP, GROUP)
            ref[zh // 2][:, span] = cotangent[:, pl.ds(start, GROUP)]
        start = pl.multiple_of((2 * zh + 1 - place[6]) * GROUP, GROUP)
        other_all[:, zh * GROUP : (zh + 1) * GROUP] = cotangent[:, pl.ds(start, GROUP)]


def split(place, cotangent):
    half = jax.ShapeDtypeStruct((CHUNK, 2 * GROUP), cotangent.dtype)
    return pl.pallas_call(
        split_kernel,
        in_specs=[pl.BlockSpec(memory_space=pltpu.SMEM), pl.BlockSpec((CHUNK, D), lambda: (0, 0))],
        out_shape=[half] * 4 + [jax.ShapeDtypeStruct((CHUNK, 4 * GROUP), cotangent.dtype)],
        name="split",
    )(place, cotangent)


def product_kernel(
    place, att_same, att_cross, own, beside, hop_one, hop_two, hop_three, last, gates, keep, send
):
    def att(which, *hops):
        ref = (att_same, att_cross)[which // 2]
        parts = []
        for at in hops:
            columns = pl.ds(pl.multiple_of(place[1 + at] * CHUNK, CHUNK), CHUNK)
            parts.append(ref[which % 2, :, columns])
        return parts[0] if len(parts) == 1 else jnp.concatenate(parts, axis=1)

    def dot(left, *blocks):
        right = blocks[0] if len(blocks) == 1 else jnp.concatenate(blocks, axis=0)
        return jnp.dot(left, right, preferred_element_type=jnp.float32)

    total = jnp.zeros((FEAT, GROUP), jnp.float32)
    for which in range(4):
        clip = dot(att(which, 1, 2), hop_one[which], hop_two[which])
        clip += dot(att(which, 3), hop_three[which])
        if which < 2:
            near = (own, beside)[which][...]
            clip += dot(att(which, 0, 4), near, last[which])
        total += gates[pl.ds(place[7 + which], 1), :] * clip
    packed = []
    for yh in range(2):
        at = yh * HB
        rest = total[at + 128 : at + HB]
        moved = pltpu.roll(rest, GROUP - HALF, 1)
        packed.append((total[at : at + 128].T, jnp.concatenate([rest, moved], axis=0).T))

    def store(ref, core):
        for yh in range(2):
            for yl in range(NY):
                at = (2 * yl + core) * LB
                ref[NY * yh + yl, 0, :LB] = packed[yh][0][at : at + LB]
                ref[NY * yh + yl, 0, LB:] = packed[yh][1][at : at + HALF]

    for core in range(2):

        @pl.when(place[0] == core)
        def _():
            store(keep, core)
            store(send, 1 - core)


def product(place, att_same, att_cross, own, beside, blocks, gates):
    count = own.shape[1] // GROUP
    attn = pl.BlockSpec((2, FEAT, TOK), lambda z: (0, 0, 0))
    plain = pl.BlockSpec((CHUNK, GROUP), lambda z: (0, z))
    four = pl.BlockSpec((4, CHUNK, GROUP), lambda z: (0, 0, z))
    pair = pl.BlockSpec((2, CHUNK, GROUP), lambda z: (0, 0, z))
    rows = pl.BlockSpec((4, GROUP), lambda z: (0, z))
    out = pl.BlockSpec((2 * NY, 1, PACK, 128), lambda z: (0, z, 0, 0))
    shape = jax.ShapeDtypeStruct((2 * NY, count, PACK, 128), jnp.float32)
    flops = 2 * 16 * CHUNK * FEAT * GROUP * count
    return pl.pallas_call(
        product_kernel,
        grid=(count,),
        in_specs=[pl.BlockSpec(memory_space=pltpu.SMEM), attn, attn, plain, plain]
        + [four, four, four, pair, rows],
        out_specs=[out, out],
        out_shape=[shape, shape],
        cost_estimate=pl.CostEstimate(flops=flops, bytes_accessed=8 << 20, transcendentals=0),
        compiler_params=pltpu.CompilerParams(vmem_limit_bytes=32 << 20),
        name="product",
    )(place, att_same, att_cross, own, beside, *blocks, gates)


def update_kernel(
    parts,
    weight,
    exp_avg,
    exp_avg_sq,
    left_stats,
    right_stats,
    left_basis,
    right_basis,
    update,
    new_weight,
    moment_out,
    second_out,
    left_new,
    right_new,
):
    def dot(left, right, dims):
        return lax.dot_general(
            left,
            right,
            (dims, ((), ())),
            precision=lax.Precision.HIGHEST,
            preferred_element_type=jnp.float32,
        )

    plain, first, last = ((1,), (0,)), ((0,), (0,)), ((1,), (1,))
    packed = jnp.sum(parts[...], axis=0)
    rest = jnp.concatenate([packed[LB:, : HB - 128], packed[LB:, HB - 128 :]], axis=0)
    gradient = jnp.concatenate([packed[:LB], rest], axis=1)
    left_q, right_q = left_basis[...], right_basis[...]
    moment = beta_one * exp_avg[...] + (1.0 - beta_one) * gradient
    moment_out[...] = moment
    rotated = dot(dot(left_q, gradient, first), right_q, plain)
    second = beta_two * exp_avg_sq[...] + (1.0 - beta_two) * rotated * rotated
    second_out[...] = second
    turned = dot(dot(left_q, moment, first), right_q, plain)
    direction = turned / (jnp.sqrt(second) + epsilon)
    step = dot(dot(left_q, direction, plain), right_q, last)
    update[...] = step
    new_weight[...] = weight[...] * (1.0 - learn_rate * decay_rate) - learn_rate * step
    left_new[...] = beta_two * left_stats[...] + (1.0 - beta_two) * dot(gradient, gradient, last)
    right_new[...] = beta_two * right_stats[...] + (1.0 - beta_two) * dot(gradient, gradient, first)


def local(
    attn_out,
    cotangent,
    gate,
    weight,
    exp_avg,
    exp_avg_sq,
    left_stats,
    right_stats,
    left_basis,
    right_basis,
):
    yh, x, zl, core = (lax.axis_index(name) for name in ("yh", "x", "zl", "c"))
    step = 1 - 2 * core
    clips = [2 * z + c for c in (core, 1 - core) for z in (zl, 1 - zl)]
    place = [core] + [lax.rem(x - step * hops + NX, NX) for hops in range(5)] + [zl] + clips
    place = jnp.stack(place)

    mine_one, mine_two, other_one, other_two, other_all = split(place, cotangent)
    rings = []
    for mine, other in ((mine_one, other_one), (mine_two, other_two)):
        blocks = [
            jnp.stack([hop(mine), hop(other, 1, 0), hop(mine, 0, 1), hop(other, 1, 1)])
        ]
        blocks.append(hop(blocks[-1]))
        blocks.append(hop(blocks[-1]))
        blocks.append(hop(blocks[-1][:2]))
        rings.append(blocks)
    beside = lax.ppermute(other_all, "zl", SWAP)

    features = attn_out.T
    kept = lax.dynamic_slice_in_dim(features, yh * TOK, TOK, 1)
    came = lax.ppermute(
        lax.dynamic_slice_in_dim(features, (1 - yh) * TOK, TOK, 1), "yh", SWAP
    )
    att_own = jnp.concatenate(
        [jnp.where(yh == 0, kept, came), jnp.where(yh == 0, came, kept)], axis=0
    )
    att_same = jnp.stack([att_own, lax.ppermute(att_own, "zl", SWAP)])
    att_cross = lax.ppermute(att_same, "c", SWAP)
    gates = lax.all_gather(gate, ("zl", "c"), axis=0, tiled=True)

    by_z = []
    for at, (zhs, mine, blocks) in enumerate(zip(PIECES, (mine_one, mine_two), rings)):
        groups = [
            lax.dynamic_slice_in_dim(gates, (2 * zh + zl) * GROUP, GROUP, 1) for zh in zhs
        ]
        near = beside[:, 2 * at * GROUP : 2 * (at + 1) * GROUP]
        keep, send = product(
            place, att_same, att_cross, mine, near, blocks, jnp.concatenate(groups, axis=1)
        )
        paired = keep + lax.ppermute(send, "c", SWAP)
        by_z.append(jnp.sum(lax.all_to_all(paired, Y, 0, 0), axis=0))
    parts = lax.all_to_all(jnp.concatenate(by_z, axis=0), "zh", 0, 0)

    block = jax.ShapeDtypeStruct((LB, HB), jnp.float32)
    return pl.pallas_call(
        update_kernel,
        out_shape=[block] * 4
        + [
            jax.ShapeDtypeStruct((LB, LB), jnp.float32),
            jax.ShapeDtypeStruct((HB, HB), jnp.float32),
        ],
        name="update",
    )(parts, weight, exp_avg, exp_avg_sq, left_stats, right_stats, left_basis, right_basis)


def solution(mesh):
    axes = ("yh", "x", "zh", "zl", "yl", "c")
    fine = Mesh(mesh.devices.reshape(2, NX, NZH, 2, NY, 2), axes)
    block = P(ROW, COL)
    in_specs = (block, P(COL + ROW, None), P(ROW, None)) + (block,) * 7
    return jax.shard_map(
        local, mesh=fine, in_specs=in_specs, out_specs=(block,) * 6, check_vma=False
    )
```

```python
import functools

import jax
import jax.numpy as jnp
from jax import lax
from jax.experimental import pallas as pl
from jax.experimental.pallas import tpu as pltpu
from jax.sharding import Mesh, PartitionSpec as P

beta_one = 0.9
beta_two = 0.95
epsilon = 1e-08
learn_rate = 0.02
decay_rate = 0.1

D = 3072
LB = 48
HB = 192
NX = 8
NZH = 4
NY = 4
CHUNK = 128
TOK = NX * CHUNK
FEAT = 2 * HB
GROUP = D // 8
HALF = LB // 2
PACK = (LB * HB) // 128
ROW = ("zh", "zl", "yl", "c")
COL = ("yh", "x")
Y = ("yh", "yl")
SWAP = [(0, 1), (1, 0)]


def at_ring(x, zl, c):
    return (x % NX) * 4 + 2 * zl + c


def ring(other_z, other_core):
    pairs = []
    for x in range(NX):
        for zl in range(2):
            for c in range(2):
                to_z, to_c = zl ^ other_z, c ^ other_core
                pairs.append((at_ring(x, zl, c), at_ring(x + 1 - 2 * to_c, to_z, to_c)))
    return pairs


def hop(block, other_z=0, other_core=0):
    return lax.ppermute(block, ("x", "zl", "c"), ring(other_z, other_core))


def after(value, *others):
    return lax.optimization_barrier((value, *others))[0]


def split_kernel(place, cotangent, mine_one, mine_two, other_one, other_two, other_all):
    for zh in range(NZH):
        span = slice((zh % 2) * GROUP, (zh % 2 + 1) * GROUP)
        for parity, ref in ((place[6], (mine_one, mine_two)), (1 - place[6], (other_one, other_two))):
            start = pl.multiple_of((2 * zh + parity) * GROUP, GROUP)
            ref[zh // 2][:, span] = cotangent[:, pl.ds(start, GROUP)]
        start = pl.multiple_of((2 * zh + 1 - place[6]) * GROUP, GROUP)
        other_all[:, zh * GROUP : (zh + 1) * GROUP] = cotangent[:, pl.ds(start, GROUP)]


def split(place, cotangent):
    half = jax.ShapeDtypeStruct((CHUNK, 2 * GROUP), cotangent.dtype)
    return pl.pallas_call(
        split_kernel,
        in_specs=[pl.BlockSpec(memory_space=pltpu.SMEM), pl.BlockSpec((CHUNK, D), lambda: (0, 0))],
        out_shape=[half] * 4 + [jax.ShapeDtypeStruct((CHUNK, 4 * GROUP), cotangent.dtype)],
        name="split",
    )(place, cotangent)


def features_kernel(place, kept, came, gate, own, cross):
    for top, bottom, yh in ((kept, came, 0), (came, kept, 1)):

        @pl.when(place[9] == yh)
        def _():
            for ref, hops, sign in ((own, range(5), 1), (cross, range(1, 4), -1)):
                for at, count in enumerate(hops):
                    start = pl.multiple_of(place[1 + (sign * count) % NX] * CHUNK, CHUNK)
                    here = slice(at * CHUNK, (at + 1) * CHUNK)
                    ref[:HB, here] = top[:, pl.ds(start, CHUNK)]
                    ref[HB:FEAT, here] = bottom[:, pl.ds(start, CHUNK)]

    rest = gate[...]
    rows = []
    for _ in range(3):
        part = rest.astype(jnp.bfloat16)
        rest = rest - part.astype(jnp.float32)
        rows.append(part)
    rows = jnp.concatenate(rows + [jnp.zeros_like(rows[0])], axis=0)
    for ref in (own, cross):
        ref[FEAT:, :GROUP] = rows
        if ref.shape[1] > GROUP:
            ref[FEAT:, GROUP:] = jnp.zeros((32, ref.shape[1] - GROUP), jnp.bfloat16)


def features_of(place, kept, came, gate):
    def shape(hops):
        return jax.ShapeDtypeStruct((FEAT + 32, hops * CHUNK), jnp.bfloat16)

    def whole(array):
        return pl.BlockSpec(array.shape, lambda: (0, 0))

    return pl.pallas_call(
        features_kernel,
        in_specs=[pl.BlockSpec(memory_space=pltpu.SMEM), whole(kept), whole(came), whole(gate)],
        out_shape=[shape(5), shape(3)],
        name="features",
    )(place, kept, came, gate)


def product_kernel(
    piece,
    place,
    att_own,
    att_beside,
    att_cross,
    att_across,
    own,
    beside,
    hop_one,
    hop_two,
    hop_three,
    last,
    keep,
    send,
):
    group = 2 * (2 * piece + pl.program_id(0)) + place[6]

    def dot(left, *blocks):
        right = blocks[0] if len(blocks) == 1 else jnp.concatenate(blocks, axis=0)
        return jnp.dot(left, right, preferred_element_type=jnp.float32)

    total = jnp.zeros((FEAT, GROUP), jnp.float32)
    for which, att in enumerate((att_own, att_beside, att_cross, att_across)):
        one, two, three = hop_one[which], hop_two[which], hop_three[which]
        if which < 2:
            near = (own, beside)[which][...]
            clip = dot(att[:FEAT, : 2 * CHUNK], near, one)
            clip += dot(att[:FEAT, 2 * CHUNK : 4 * CHUNK], two, three)
            clip += dot(att[:FEAT, 4 * CHUNK :], last[which])
        else:
            clip = dot(att[:FEAT, : 2 * CHUNK], one, two)
            clip += dot(att[:FEAT, 2 * CHUNK :], three)
        parts = att[FEAT:, :GROUP].astype(jnp.float32)
        rows = lax.broadcasted_iota(jnp.int32, parts.shape, 0)
        mine = (rows & 7 == group) & (rows < 24)
        gate = jnp.sum(jnp.where(mine, parts, 0.0), axis=0, keepdims=True)
        total += gate * clip
    packed = []
    for yh in range(2):
        at = yh * HB
        rest = total[at + 128 : at + HB]
        moved = pltpu.roll(rest, GROUP - HALF, 1)
        packed.append((total[at : at + 128].T, jnp.concatenate([rest, moved], axis=0).T))

    def store(ref, core):
        for yh in range(2):
            for yl in range(NY):
                at = (2 * yl + core) * LB
                ref[NY * yh + yl, 0, :LB] = packed[yh][0][at : at + LB]
                ref[NY * yh + yl, 0, LB:] = packed[yh][1][at : at + HALF]

    for core in range(2):

        @pl.when(place[0] == core)
        def _():
            store(keep, core)
            store(send, 1 - core)


def product(piece, place, atts, own, beside, blocks):
    count = own.shape[1] // GROUP
    attn = [pl.BlockSpec(att.shape, lambda z: (0, 0)) for att in atts]
    plain = pl.BlockSpec((CHUNK, GROUP), lambda z: (0, z))
    near = pl.BlockSpec((CHUNK, GROUP), lambda z: (0, 2 * piece + z))
    four = pl.BlockSpec((4, CHUNK, GROUP), lambda z: (0, 0, z))
    pair = pl.BlockSpec((2, CHUNK, GROUP), lambda z: (0, 0, z))
    out = pl.BlockSpec((2 * NY, 1, PACK, 128), lambda z: (0, z, 0, 0))
    shape = jax.ShapeDtypeStruct((2 * NY, count, PACK, 128), jnp.float32)
    flops = 2 * 16 * CHUNK * FEAT * GROUP * count
    return pl.pallas_call(
        functools.partial(product_kernel, piece),
        grid=(count,),
        in_specs=[pl.BlockSpec(memory_space=pltpu.SMEM)]
        + attn
        + [plain, near, four, four, four, pair],
        out_specs=[out, out],
        out_shape=[shape, shape],
        cost_estimate=pl.CostEstimate(flops=flops, bytes_accessed=8 << 20, transcendentals=0),
        compiler_params=pltpu.CompilerParams(vmem_limit_bytes=32 << 20),
        name="product",
    )(place, *atts, own, beside, *blocks)


def update_kernel(
    parts,
    weight,
    exp_avg,
    exp_avg_sq,
    left_stats,
    right_stats,
    left_basis,
    right_basis,
    update,
    new_weight,
    moment_out,
    second_out,
    left_new,
    right_new,
):
    def dot(left, right, dims):
        return lax.dot_general(
            left,
            right,
            (dims, ((), ())),
            precision=lax.Precision.HIGHEST,
            preferred_element_type=jnp.float32,
        )

    plain, first, last = ((1,), (0,)), ((0,), (0,)), ((1,), (1,))
    packed = jnp.sum(parts[...], axis=0)
    rest = jnp.concatenate([packed[LB:, : HB - 128], packed[LB:, HB - 128 :]], axis=0)
    gradient = jnp.concatenate([packed[:LB], rest], axis=1)
    left_q, right_q = left_basis[...], right_basis[...]
    moment = beta_one * exp_avg[...] + (1.0 - beta_one) * gradient
    moment_out[...] = moment
    rotated = dot(dot(left_q, gradient, first), right_q, plain)
    second = beta_two * exp_avg_sq[...] + (1.0 - beta_two) * rotated * rotated
    second_out[...] = second
    turned = dot(dot(left_q, moment, first), right_q, plain)
    direction = turned / (jnp.sqrt(second) + epsilon)
    step = dot(dot(left_q, direction, plain), right_q, last)
    update[...] = step
    new_weight[...] = weight[...] * (1.0 - learn_rate * decay_rate) - learn_rate * step
    left_new[...] = beta_two * left_stats[...] + (1.0 - beta_two) * dot(gradient, gradient, last)
    right_new[...] = beta_two * right_stats[...] + (1.0 - beta_two) * dot(gradient, gradient, first)


def local(
    attn_out,
    cotangent,
    gate,
    weight,
    exp_avg,
    exp_avg_sq,
    left_stats,
    right_stats,
    left_basis,
    right_basis,
):
    yh, x, zl, core = (lax.axis_index(name) for name in ("yh", "x", "zl", "c"))
    step = 1 - 2 * core
    sources = [lax.rem(x - step * count + 2 * NX, NX) for count in range(NX)]
    place = jnp.stack([core] + sources[:5] + [zl])

    mine_one, mine_two, other_one, other_two, other_all = split(place, cotangent)

    def first_hop(mine, other):
        return [hop(mine), hop(other, 1, 0), hop(mine, 0, 1), hop(other, 1, 1)]

    parts_one = first_hop(mine_one, other_one)
    parts_two = first_hop(after(mine_two, parts_one[0]), after(other_two, parts_one[0]))
    first_one = jnp.stack(parts_one)
    first_two = jnp.stack(parts_two)

    features = attn_out.T
    kept = lax.dynamic_slice_in_dim(features, yh * TOK, TOK, 1)
    away = lax.dynamic_slice_in_dim(features, (1 - yh) * TOK, TOK, 1)
    came = after(lax.ppermute(after(away, parts_one[0]), "yh", SWAP), first_two)
    att_own, att_swap = features_of(jnp.stack([core] + sources + [yh]), kept, came, gate.reshape(8, GROUP))
    atts = (
        att_own,
        lax.ppermute(att_own, "zl", SWAP),
        lax.ppermute(att_swap, "c", SWAP),
        lax.ppermute(att_swap, ("zl", "c"), [(0, 3), (1, 2), (2, 1), (3, 0)]),
    )

    second_one = hop(first_one)
    second_two = hop(first_two)
    third_one = hop(after(second_one, first_two, att_own))
    third_two = hop(second_two)
    last_one = hop(after(third_one, second_two)[:2])
    last_two = hop(third_two[:2])
    beside = lax.ppermute(after(other_all, second_two), "zl", SWAP)
    rings = (
        (mine_one, (first_one, second_one, third_one, last_one)),
        (mine_two, (first_two, second_two, third_two, last_two)),
    )

    by_z = []
    for at, (mine, blocks) in enumerate(rings):
        keep, send = product(at, place, atts, mine, beside, blocks)
        paired = keep + lax.ppermute(send, "c", SWAP)
        by_z.append(jnp.sum(lax.all_to_all(paired, Y, 0, 0), axis=0))
    parts = lax.all_to_all(jnp.concatenate(by_z, axis=0), "zh", 0, 0)

    block = jax.ShapeDtypeStruct((LB, HB), jnp.float32)
    return pl.pallas_call(
        update_kernel,
        out_shape=[block] * 4
        + [
            jax.ShapeDtypeStruct((LB, LB), jnp.float32),
            jax.ShapeDtypeStruct((HB, HB), jnp.float32),
        ],
        name="update",
    )(parts, weight, exp_avg, exp_avg_sq, left_stats, right_stats, left_basis, right_basis)


def solution(mesh):
    axes = ("yh", "x", "zh", "zl", "yl", "c")
    fine = Mesh(mesh.devices.reshape(2, NX, NZH, 2, NY, 2), axes)
    block = P(ROW, COL)
    in_specs = (block, P(COL + ROW, None), P(ROW, None)) + (block,) * 7
    return jax.shard_map(
        local, mesh=fine, in_specs=in_specs, out_specs=(block,) * 6, check_vma=False
    )
```

```python
import functools

import jax
import jax.numpy as jnp
from jax import lax
from jax.experimental import pallas as pl
from jax.experimental.pallas import tpu as pltpu
from jax.sharding import Mesh, PartitionSpec as P

beta_one = 0.9
beta_two = 0.95
epsilon = 1e-08
learn_rate = 0.02
decay_rate = 0.1

D = 3072
LB = 48
HB = 192
NX = 8
NZH = 4
NY = 4
CHUNK = 128
TOK = NX * CHUNK
FEAT = 2 * HB
GROUP = D // 8
HALF = LB // 2
PACK = (LB * HB) // 128
ROW = ("zh", "zl", "yl", "c")
COL = ("yh", "x")
Y = ("yh", "yl")
SWAP = [(0, 1), (1, 0)]


def at_ring(x, zl, c):
    return (x % NX) * 4 + 2 * zl + c


def ring(other_z, other_core):
    pairs = []
    for x in range(NX):
        for zl in range(2):
            for c in range(2):
                to_z, to_c = zl ^ other_z, c ^ other_core
                pairs.append((at_ring(x, zl, c), at_ring(x + 1 - 2 * to_c, to_z, to_c)))
    return pairs


def hop(block, other_z=0, other_core=0):
    return lax.ppermute(block, ("x", "zl", "c"), ring(other_z, other_core))


def after(value, *others):
    return lax.optimization_barrier((value, *others))[0]


def split_kernel(place, cotangent, mine, other):
    for zh in range(NZH):
        for parity, ref in ((place[10], mine), (1 - place[10], other)):
            start = pl.multiple_of((2 * zh + parity) * GROUP, GROUP)
            at = (zh % 2) * GROUP
            ref[zh // 2, :, at : at + GROUP] = cotangent[:, pl.ds(start, GROUP)]


def split(place, cotangent):
    half = jax.ShapeDtypeStruct((2, CHUNK, D // 4), cotangent.dtype)
    return pl.pallas_call(
        split_kernel,
        in_specs=[pl.BlockSpec(memory_space=pltpu.SMEM), pl.BlockSpec((CHUNK, D), lambda: (0, 0))],
        out_shape=[half] * 2,
        name="split",
    )(place, cotangent)


def features_kernel(place, kept, came, gate, own, cross):
    for top, bottom, yh in ((kept, came, 0), (came, kept, 1)):

        @pl.when(place[9] == yh)
        def _():
            for ref, hops, sign in ((own, range(5), 1), (cross, range(1, 4), -1)):
                for at, count in enumerate(hops):
                    start = pl.multiple_of(place[1 + (sign * count) % NX] * CHUNK, CHUNK)
                    here = slice(at * CHUNK, (at + 1) * CHUNK)
                    ref[:HB, here] = top[:, pl.ds(start, CHUNK)]
                    ref[HB:FEAT, here] = bottom[:, pl.ds(start, CHUNK)]

    rest = jnp.concatenate([gate[:, z * GROUP : (z + 1) * GROUP] for z in range(8)], axis=0)
    rows = []
    for _ in range(3):
        part = rest.astype(jnp.bfloat16)
        rest = rest - part.astype(jnp.float32)
        rows.append(part)
    rows = jnp.concatenate(rows + [jnp.zeros_like(rows[0])], axis=0)
    for ref in (own, cross):
        ref[FEAT:, :GROUP] = rows
        if ref.shape[1] > GROUP:
            ref[FEAT:, GROUP:] = jnp.zeros((32, ref.shape[1] - GROUP), jnp.bfloat16)


def features_of(place, kept, came, gate):
    def shape(hops):
        return jax.ShapeDtypeStruct((FEAT + 32, hops * CHUNK), jnp.bfloat16)

    def whole(array):
        return pl.BlockSpec(array.shape, lambda: (0, 0))

    return pl.pallas_call(
        features_kernel,
        in_specs=[pl.BlockSpec(memory_space=pltpu.SMEM), whole(kept), whole(came), whole(gate)],
        out_shape=[shape(5), shape(3)],
        name="features",
    )(place, kept, came, gate)


def product_kernel(
    piece,
    place,
    att_own,
    att_beside,
    att_cross,
    att_across,
    own,
    beside,
    hop_one,
    hop_two,
    hop_three,
    last,
    keep,
    send,
):
    group = 2 * (2 * piece + pl.program_id(0)) + place[10]

    def dot(left, *blocks):
        right = blocks[0] if len(blocks) == 1 else jnp.concatenate(blocks, axis=0)
        return jnp.dot(left, right, preferred_element_type=jnp.float32)

    total = jnp.zeros((FEAT, GROUP), jnp.float32)
    for which, att in enumerate((att_own, att_beside, att_cross, att_across)):
        one, two, three = hop_one[which], hop_two[which], hop_three[which]
        if which < 2:
            near = (own, beside)[which][0]
            clip = dot(att[:FEAT, : 2 * CHUNK], near, one)
            clip += dot(att[:FEAT, 2 * CHUNK : 4 * CHUNK], two, three)
            clip += dot(att[:FEAT, 4 * CHUNK :], last[which])
        else:
            clip = dot(att[:FEAT, : 2 * CHUNK], one, two)
            clip += dot(att[:FEAT, 2 * CHUNK :], three)
        parts = att[FEAT:, :GROUP].astype(jnp.float32)
        rows = lax.broadcasted_iota(jnp.int32, parts.shape, 0)
        mine = (rows & 7 == group) & (rows < 24)
        gate = jnp.sum(jnp.where(mine, parts, 0.0), axis=0, keepdims=True)
        total += gate * clip
    packed = []
    for yh in range(2):
        at = yh * HB
        rest = total[at + 128 : at + HB]
        moved = pltpu.roll(rest, GROUP - HALF, 1)
        packed.append((total[at : at + 128].T, jnp.concatenate([rest, moved], axis=0).T))

    def store(ref, core):
        for yh in range(2):
            for yl in range(NY):
                at = (2 * yl + core) * LB
                ref[NY * yh + yl, 0, :LB] = packed[yh][0][at : at + LB]
                ref[NY * yh + yl, 0, LB:] = packed[yh][1][at : at + HALF]

    for core in range(2):

        @pl.when(place[0] == core)
        def _():
            store(keep, core)
            store(send, 1 - core)


def product(piece, place, atts, own, beside, blocks):
    count = blocks[0].shape[2] // GROUP
    attn = [pl.BlockSpec(att.shape, lambda z: (0, 0)) for att in atts]
    near = pl.BlockSpec((1, CHUNK, GROUP), lambda z: (piece, 0, z))
    four = pl.BlockSpec((4, CHUNK, GROUP), lambda z: (0, 0, z))
    pair = pl.BlockSpec((2, CHUNK, GROUP), lambda z: (0, 0, z))
    out = pl.BlockSpec((2 * NY, 1, PACK, 128), lambda z: (0, z, 0, 0))
    shape = jax.ShapeDtypeStruct((2 * NY, count, PACK, 128), jnp.float32)
    flops = 2 * 16 * CHUNK * FEAT * GROUP * count
    return pl.pallas_call(
        functools.partial(product_kernel, piece),
        grid=(count,),
        in_specs=[pl.BlockSpec(memory_space=pltpu.SMEM)]
        + attn
        + [near, near, four, four, four, pair],
        out_specs=[out, out],
        out_shape=[shape, shape],
        cost_estimate=pl.CostEstimate(flops=flops, bytes_accessed=8 << 20, transcendentals=0),
        compiler_params=pltpu.CompilerParams(vmem_limit_bytes=32 << 20),
        name="product",
    )(place, *atts, own, beside, *blocks)


def update_kernel(
    parts,
    weight,
    exp_avg,
    exp_avg_sq,
    left_stats,
    right_stats,
    left_basis,
    right_basis,
    update,
    new_weight,
    moment_out,
    second_out,
    left_new,
    right_new,
):
    def dot(left, right, dims):
        return lax.dot_general(
            left,
            right,
            (dims, ((), ())),
            precision=lax.Precision.HIGHEST,
            preferred_element_type=jnp.float32,
        )

    plain, first, last = ((1,), (0,)), ((0,), (0,)), ((1,), (1,))
    packed = jnp.sum(parts[...], axis=0)
    rest = jnp.concatenate([packed[LB:, : HB - 128], packed[LB:, HB - 128 :]], axis=0)
    gradient = jnp.concatenate([packed[:LB], rest], axis=1)
    left_q, right_q = left_basis[...], right_basis[...]
    moment = beta_one * exp_avg[...] + (1.0 - beta_one) * gradient
    moment_out[...] = moment
    rotated = dot(dot(left_q, gradient, first), right_q, plain)
    second = beta_two * exp_avg_sq[...] + (1.0 - beta_two) * rotated * rotated
    second_out[...] = second
    turned = dot(dot(left_q, moment, first), right_q, plain)
    direction = turned / (jnp.sqrt(second) + epsilon)
    step = dot(dot(left_q, direction, plain), right_q, last)
    update[...] = step
    new_weight[...] = weight[...] * (1.0 - learn_rate * decay_rate) - learn_rate * step
    left_new[...] = beta_two * left_stats[...] + (1.0 - beta_two) * dot(gradient, gradient, last)
    right_new[...] = beta_two * right_stats[...] + (1.0 - beta_two) * dot(gradient, gradient, first)


def local(
    attn_out,
    cotangent,
    gate,
    weight,
    exp_avg,
    exp_avg_sq,
    left_stats,
    right_stats,
    left_basis,
    right_basis,
):
    yh, x, zl, core = (lax.axis_index(name) for name in ("yh", "x", "zl", "c"))
    step = 1 - 2 * core
    sources = [lax.rem(x - step * count + 2 * NX, NX) for count in range(NX)]
    place = jnp.stack([core] + sources + [yh, zl])

    features = attn_out.T
    kept = lax.dynamic_slice_in_dim(features, yh * TOK, TOK, 1)
    away = lax.dynamic_slice_in_dim(features, (1 - yh) * TOK, TOK, 1)
    came = lax.ppermute(away, "yh", SWAP)

    mine, other = split(place, cotangent)
    parts = [hop(mine), hop(other, 1, 0), hop(mine, 0, 1), hop(other, 1, 1)]
    first_one = jnp.stack([part[0] for part in parts])
    first_two = jnp.stack([part[1] for part in parts])
    second_one = hop(after(first_one, came))
    second_two = hop(after(first_two, came))

    att_own, att_swap = features_of(place, kept, after(came, first_two), gate)
    atts = (
        att_own,
        lax.ppermute(att_own, "zl", SWAP),
        lax.ppermute(att_swap, "c", SWAP),
        lax.ppermute(att_swap, ("zl", "c"), [(0, 3), (1, 2), (2, 1), (3, 0)]),
    )

    third_one = hop(after(second_one, att_own))
    third_two = hop(second_two)
    last_one = hop(after(third_one, second_two)[:2])
    last_two = hop(third_two[:2])
    beside = lax.ppermute(after(other, second_one), "zl", SWAP)
    rings = (
        (first_one, second_one, third_one, last_one),
        (first_two, second_two, third_two, last_two),
    )

    by_z = []
    for at, blocks in enumerate(rings):
        keep, send = product(at, place, atts, mine, beside, blocks)
        paired = keep + lax.ppermute(send, "c", SWAP)
        by_z.append(jnp.sum(lax.all_to_all(paired, Y, 0, 0), axis=0))
    parts = lax.all_to_all(jnp.concatenate(by_z, axis=0), "zh", 0, 0)

    block = jax.ShapeDtypeStruct((LB, HB), jnp.float32)
    return pl.pallas_call(
        update_kernel,
        out_shape=[block] * 4
        + [
            jax.ShapeDtypeStruct((LB, LB), jnp.float32),
            jax.ShapeDtypeStruct((HB, HB), jnp.float32),
        ],
        name="update",
    )(parts, weight, exp_avg, exp_avg_sq, left_stats, right_stats, left_basis, right_basis)


def solution(mesh):
    axes = ("yh", "x", "zh", "zl", "yl", "c")
    fine = Mesh(mesh.devices.reshape(2, NX, NZH, 2, NY, 2), axes)
    block = P(ROW, COL)
    in_specs = (block, P(COL + ROW, None), P(ROW, None)) + (block,) * 7
    return jax.shard_map(
        local, mesh=fine, in_specs=in_specs, out_specs=(block,) * 6, check_vma=False
    )
```

```python
import functools

import jax
import jax.numpy as jnp
from jax import lax
from jax.experimental import pallas as pl
from jax.experimental.pallas import tpu as pltpu
from jax.sharding import Mesh, PartitionSpec as P

beta_one = 0.9
beta_two = 0.95
epsilon = 1e-08
learn_rate = 0.02
decay_rate = 0.1

D = 3072
LB = 48
HB = 192
NX = 8
NZH = 4
NY = 4
CHUNK = 128
TOK = NX * CHUNK
FEAT = 2 * HB
GROUP = D // 8
HALF = LB // 2
PACK = (LB * HB) // 128
ROW = ("zh", "zl", "yl", "c")
COL = ("yh", "x")
Y = ("yh", "yl")
SWAP = [(0, 1), (1, 0)]


def at_ring(x, zl, c):
    return (x % NX) * 4 + 2 * zl + c


def ring(other_z, other_core):
    pairs = []
    for x in range(NX):
        for zl in range(2):
            for c in range(2):
                to_z, to_c = zl ^ other_z, c ^ other_core
                pairs.append((at_ring(x, zl, c), at_ring(x + 1 - 2 * to_c, to_z, to_c)))
    return pairs


def hop(block, other_z=0, other_core=0):
    return lax.ppermute(block, ("x", "zl", "c"), ring(other_z, other_core))


def after(value, *others):
    return lax.optimization_barrier((value, *others))[0]


def split_kernel(place, cotangent, mine, other):
    for zh in range(NZH):
        for parity, ref in ((place[10], mine), (1 - place[10], other)):
            start = pl.multiple_of((2 * zh + parity) * GROUP, GROUP)
            at = (zh % 2) * GROUP
            ref[zh // 2, :, at : at + GROUP] = cotangent[:, pl.ds(start, GROUP)]


def split(place, cotangent):
    half = jax.ShapeDtypeStruct((2, CHUNK, D // 4), cotangent.dtype)
    return pl.pallas_call(
        split_kernel,
        in_specs=[pl.BlockSpec(memory_space=pltpu.SMEM), pl.BlockSpec((CHUNK, D), lambda: (0, 0))],
        out_shape=[half] * 2,
        name="split",
    )(place, cotangent)


def features_kernel(place, kept, came, gate, own, cross):
    for top, bottom, yh in ((kept, came, 0), (came, kept, 1)):

        @pl.when(place[9] == yh)
        def _():
            for ref, hops, sign in ((own, range(5), 1), (cross, range(1, 4), -1)):
                for at, count in enumerate(hops):
                    start = pl.multiple_of(place[1 + (sign * count) % NX] * CHUNK, CHUNK)
                    here = slice(at * CHUNK, (at + 1) * CHUNK)
                    ref[:HB, here] = top[:, pl.ds(start, CHUNK)]
                    ref[HB:FEAT, here] = bottom[:, pl.ds(start, CHUNK)]

    rest = jnp.concatenate([gate[:, z * GROUP : (z + 1) * GROUP] for z in range(8)], axis=0)
    rows = []
    for _ in range(3):
        part = rest.astype(jnp.bfloat16)
        rest = rest - part.astype(jnp.float32)
        rows.append(part)
    rows = jnp.concatenate(rows + [jnp.zeros_like(rows[0])], axis=0)
    for ref in (own, cross):
        ref[FEAT:, :GROUP] = rows
        if ref.shape[1] > GROUP:
            ref[FEAT:, GROUP:] = jnp.zeros((32, ref.shape[1] - GROUP), jnp.bfloat16)


def features_of(place, kept, came, gate):
    def shape(hops):
        return jax.ShapeDtypeStruct((FEAT + 32, hops * CHUNK), jnp.bfloat16)

    def whole(array):
        return pl.BlockSpec(array.shape, lambda: (0, 0))

    return pl.pallas_call(
        features_kernel,
        in_specs=[pl.BlockSpec(memory_space=pltpu.SMEM), whole(kept), whole(came), whole(gate)],
        out_shape=[shape(5), shape(3)],
        name="features",
    )(place, kept, came, gate)


def product_kernel(
    piece,
    place,
    att_own,
    att_beside,
    att_cross,
    att_across,
    own,
    beside,
    hop_one,
    hop_two,
    hop_three,
    last,
    keep,
    send,
):
    group = 2 * (2 * piece + pl.program_id(0)) + place[10]

    def dot(left, *blocks):
        right = blocks[0] if len(blocks) == 1 else jnp.concatenate(blocks, axis=0)
        return jnp.dot(left, right, preferred_element_type=jnp.float32)

    total = jnp.zeros((FEAT, GROUP), jnp.float32)
    for which, att in enumerate((att_own, att_beside, att_cross, att_across)):
        one, two, three = hop_one[which], hop_two[which], hop_three[which]
        if which < 2:
            near = (own, beside)[which][0]
            clip = dot(att[:FEAT, : 2 * CHUNK], near, one)
            clip += dot(att[:FEAT, 2 * CHUNK : 4 * CHUNK], two, three)
            clip += dot(att[:FEAT, 4 * CHUNK :], last[which])
        else:
            clip = dot(att[:FEAT, : 2 * CHUNK], one, two)
            clip += dot(att[:FEAT, 2 * CHUNK :], three)
        parts = att[FEAT:, :GROUP].astype(jnp.float32)
        rows = lax.broadcasted_iota(jnp.int32, parts.shape, 0)
        mine = (rows & 7 == group) & (rows < 24)
        gate = jnp.sum(jnp.where(mine, parts, 0.0), axis=0, keepdims=True)
        total += gate * clip
    packed = []
    for yh in range(2):
        at = yh * HB
        rest = total[at + 128 : at + HB]
        moved = pltpu.roll(rest, GROUP - HALF, 1)
        packed.append((total[at : at + 128].T, jnp.concatenate([rest, moved], axis=0).T))

    def store(ref, core):
        for yh in range(2):
            for yl in range(NY):
                at = (2 * yl + core) * LB
                ref[NY * yh + yl, 0, :LB] = packed[yh][0][at : at + LB]
                ref[NY * yh + yl, 0, LB:] = packed[yh][1][at : at + HALF]

    for core in range(2):

        @pl.when(place[0] == core)
        def _():
            store(keep, core)
            store(send, 1 - core)


def product(piece, place, atts, own, beside, blocks):
    count = blocks[0].shape[2] // GROUP
    attn = [pl.BlockSpec(att.shape, lambda z: (0, 0)) for att in atts]
    near = pl.BlockSpec((1, CHUNK, GROUP), lambda z: (piece, 0, z))
    four = pl.BlockSpec((4, CHUNK, GROUP), lambda z: (0, 0, z))
    pair = pl.BlockSpec((2, CHUNK, GROUP), lambda z: (0, 0, z))
    out = pl.BlockSpec((2 * NY, 1, PACK, 128), lambda z: (0, z, 0, 0))
    shape = jax.ShapeDtypeStruct((2 * NY, count, PACK, 128), jnp.float32)
    flops = 2 * 16 * CHUNK * FEAT * GROUP * count
    return pl.pallas_call(
        functools.partial(product_kernel, piece),
        grid=(count,),
        in_specs=[pl.BlockSpec(memory_space=pltpu.SMEM)]
        + attn
        + [near, near, four, four, four, pair],
        out_specs=[out, out],
        out_shape=[shape, shape],
        cost_estimate=pl.CostEstimate(flops=flops, bytes_accessed=8 << 20, transcendentals=0),
        compiler_params=pltpu.CompilerParams(vmem_limit_bytes=32 << 20),
        name="product",
    )(place, *atts, own, beside, *blocks)


def update_kernel(
    parts,
    weight,
    exp_avg,
    exp_avg_sq,
    left_stats,
    right_stats,
    left_basis,
    right_basis,
    update,
    new_weight,
    moment_out,
    second_out,
    left_new,
    right_new,
):
    def dot(left, right, dims):
        return lax.dot_general(
            left,
            right,
            (dims, ((), ())),
            precision=lax.Precision.HIGHEST,
            preferred_element_type=jnp.float32,
        )

    plain, first, last = ((1,), (0,)), ((0,), (0,)), ((1,), (1,))
    packed = jnp.sum(parts[...], axis=0)
    rest = jnp.concatenate([packed[LB:, : HB - 128], packed[LB:, HB - 128 :]], axis=0)
    gradient = jnp.concatenate([packed[:LB], rest], axis=1)
    left_q, right_q = left_basis[...], right_basis[...]
    moment = beta_one * exp_avg[...] + (1.0 - beta_one) * gradient
    moment_out[...] = moment
    rotated = dot(dot(left_q, gradient, first), right_q, plain)
    second = beta_two * exp_avg_sq[...] + (1.0 - beta_two) * rotated * rotated
    second_out[...] = second
    turned = dot(dot(left_q, moment, first), right_q, plain)
    direction = turned / (jnp.sqrt(second) + epsilon)
    step = dot(dot(left_q, direction, plain), right_q, last)
    update[...] = step
    new_weight[...] = weight[...] * (1.0 - learn_rate * decay_rate) - learn_rate * step
    left_new[...] = beta_two * left_stats[...] + (1.0 - beta_two) * dot(gradient, gradient, last)
    right_new[...] = beta_two * right_stats[...] + (1.0 - beta_two) * dot(gradient, gradient, first)


def local(
    attn_out,
    cotangent,
    gate,
    weight,
    exp_avg,
    exp_avg_sq,
    left_stats,
    right_stats,
    left_basis,
    right_basis,
):
    yh, x, zl, core = (lax.axis_index(name) for name in ("yh", "x", "zl", "c"))
    step = 1 - 2 * core
    sources = [lax.rem(x - step * count + 2 * NX, NX) for count in range(NX)]
    place = jnp.stack([core] + sources + [yh, zl])

    features = attn_out.T
    kept = lax.dynamic_slice_in_dim(features, yh * TOK, TOK, 1)
    away = lax.dynamic_slice_in_dim(features, (1 - yh) * TOK, TOK, 1)
    came = lax.ppermute(away, "yh", SWAP)

    mine, other = split(place, cotangent)
    parts = [hop(mine), hop(other, 1, 0), hop(mine, 0, 1), hop(other, 1, 1)]
    parts = [after(part, came) for part in parts]
    first_one = jnp.stack([part[0] for part in parts])
    first_two = jnp.stack([part[1] for part in parts])
    second_one = hop(first_one)
    second_two = hop(first_two)

    att_own, att_swap = features_of(place, kept, after(came, first_two), gate)
    atts = (
        att_own,
        lax.ppermute(att_own, "zl", SWAP),
        lax.ppermute(att_swap, "c", SWAP),
        lax.ppermute(att_swap, ("zl", "c"), [(0, 3), (1, 2), (2, 1), (3, 0)]),
    )

    beside = lax.ppermute(after(other, first_two), "zl", SWAP)
    third_one = hop(after(second_one, first_two, att_own))
    third_two = hop(after(second_two, third_one, atts[1]))
    last_one = after(hop(after(third_one, second_two, beside)[:2]), third_two)
    last_two = hop(third_two[:2])
    rings = (
        (first_one, second_one, third_one, last_one),
        (first_two, second_two, third_two, last_two),
    )

    by_z = []
    for at, blocks in enumerate(rings):
        keep, send = product(at, place, atts, mine, beside, blocks)
        paired = keep + lax.ppermute(send, "c", SWAP)
        by_z.append(jnp.sum(lax.all_to_all(paired, Y, 0, 0), axis=0))
    parts = lax.all_to_all(jnp.concatenate(by_z, axis=0), "zh", 0, 0)

    block = jax.ShapeDtypeStruct((LB, HB), jnp.float32)
    return pl.pallas_call(
        update_kernel,
        out_shape=[block] * 4
        + [
            jax.ShapeDtypeStruct((LB, LB), jnp.float32),
            jax.ShapeDtypeStruct((HB, HB), jnp.float32),
        ],
        name="update",
    )(parts, weight, exp_avg, exp_avg_sq, left_stats, right_stats, left_basis, right_basis)


def solution(mesh):
    axes = ("yh", "x", "zh", "zl", "yl", "c")
    fine = Mesh(mesh.devices.reshape(2, NX, NZH, 2, NY, 2), axes)
    block = P(ROW, COL)
    in_specs = (block, P(COL + ROW, None), P(ROW, None)) + (block,) * 7
    return jax.shard_map(
        local, mesh=fine, in_specs=in_specs, out_specs=(block,) * 6, check_vma=False
    )
```

```python
import functools

import jax
import jax.numpy as jnp
from jax import lax
from jax.experimental import pallas as pl
from jax.experimental.pallas import tpu as pltpu
from jax.sharding import Mesh, PartitionSpec as P

beta_one = 0.9
beta_two = 0.95
epsilon = 1e-08
learn_rate = 0.02
decay_rate = 0.1

D = 3072
LB = 48
HB = 192
NX = 8
NZH = 4
NY = 4
CHUNK = 128
TOK = NX * CHUNK
FEAT = 2 * HB
GROUP = D // 8
HALF = LB // 2
PACK = (LB * HB) // 128
ROW = ("zh", "zl", "yl", "c")
COL = ("yh", "x")
Y = ("yh", "yl")
SWAP = [(0, 1), (1, 0)]


def ring(other_core):
    pairs = []
    for x in range(NX):
        for c in range(2):
            to = c ^ other_core
            pairs.append((2 * x + c, 2 * ((x + 1 - 2 * to) % NX) + to))
    return pairs


def hop(block, other_core=0):
    return lax.ppermute(block, ("x", "c"), ring(other_core))


def after(value, *others):
    return lax.optimization_barrier((value, *others))[0]


def split_kernel(place, cotangent, mine_one, mine_two, other_one, other_two):
    for parity, refs in ((place[10], (mine_one, mine_two)), (1 - place[10], (other_one, other_two))):
        for zh in range(NZH):
            start = pl.multiple_of((2 * zh + parity) * GROUP, GROUP)
            at = (zh % 2) * GROUP
            refs[zh // 2][:, at : at + GROUP] = cotangent[:, pl.ds(start, GROUP)]


def split(place, cotangent):
    piece = jax.ShapeDtypeStruct((CHUNK, D // 4), cotangent.dtype)
    return pl.pallas_call(
        split_kernel,
        in_specs=[pl.BlockSpec(memory_space=pltpu.SMEM), pl.BlockSpec((CHUNK, D), lambda: (0, 0))],
        out_shape=[piece] * 4,
        name="split",
    )(place, cotangent)


def features_kernel(place, kept, came, gate, own, cross):
    for top, bottom, yh in ((kept, came, 0), (came, kept, 1)):

        @pl.when(place[9] == yh)
        def _():
            for ref, hops, sign in ((own, range(5), 1), (cross, range(1, 4), -1)):
                for at, count in enumerate(hops):
                    start = pl.multiple_of(place[1 + (sign * count) % NX] * CHUNK, CHUNK)
                    here = slice(at * CHUNK, (at + 1) * CHUNK)
                    ref[:HB, here] = top[:, pl.ds(start, CHUNK)]
                    ref[HB:FEAT, here] = bottom[:, pl.ds(start, CHUNK)]

    rest = jnp.concatenate([gate[:, z * GROUP : (z + 1) * GROUP] for z in range(8)], axis=0)
    rows = []
    for _ in range(3):
        part = rest.astype(jnp.bfloat16)
        rest = rest - part.astype(jnp.float32)
        rows.append(part)
    rows = jnp.concatenate(rows + [jnp.zeros_like(rows[0])], axis=0)
    for ref in (own, cross):
        ref[FEAT:, :GROUP] = rows
        if ref.shape[1] > GROUP:
            ref[FEAT:, GROUP:] = jnp.zeros((32, ref.shape[1] - GROUP), jnp.bfloat16)


def features_of(place, kept, came, gate):
    def shape(hops):
        return jax.ShapeDtypeStruct((FEAT + 32, hops * CHUNK), jnp.bfloat16)

    def whole(array):
        return pl.BlockSpec(array.shape, lambda: (0, 0))

    return pl.pallas_call(
        features_kernel,
        in_specs=[pl.BlockSpec(memory_space=pltpu.SMEM), whole(kept), whole(came), whole(gate)],
        out_shape=[shape(5), shape(3)],
        name="features",
    )(place, kept, came, gate)


def product_kernel(
    piece,
    place,
    att_own,
    att_beside,
    att_cross,
    att_across,
    local_pair,
    hop_one,
    hop_two,
    hop_three,
    last,
    keep,
    send,
):
    group = 2 * (2 * piece + pl.program_id(0)) + place[10]

    def dot(left, *blocks):
        right = blocks[0] if len(blocks) == 1 else jnp.concatenate(blocks, axis=0)
        return jnp.dot(left, right, preferred_element_type=jnp.float32)

    total = jnp.zeros((FEAT, GROUP), jnp.float32)
    for which, att in enumerate((att_own, att_beside, att_cross, att_across)):
        one, two, three = hop_one[which], hop_two[which], hop_three[which]
        if which < 2:
            clip = dot(att[:FEAT, : 2 * CHUNK], local_pair[which], one)
            clip += dot(att[:FEAT, 2 * CHUNK : 4 * CHUNK], two, three)
            clip += dot(att[:FEAT, 4 * CHUNK :], last[which])
        else:
            clip = dot(att[:FEAT, : 2 * CHUNK], one, two)
            clip += dot(att[:FEAT, 2 * CHUNK :], three)
        parts = att[FEAT:, :GROUP].astype(jnp.float32)
        rows = lax.broadcasted_iota(jnp.int32, parts.shape, 0)
        mine = (rows & 7 == group) & (rows < 24)
        gate = jnp.sum(jnp.where(mine, parts, 0.0), axis=0, keepdims=True)
        total += gate * clip
    packed = []
    for yh in range(2):
        at = yh * HB
        rest = total[at + 128 : at + HB]
        moved = pltpu.roll(rest, GROUP - HALF, 1)
        packed.append((total[at : at + 128].T, jnp.concatenate([rest, moved], axis=0).T))

    def store(ref, core):
        for yh in range(2):
            for yl in range(NY):
                at = (2 * yl + core) * LB
                ref[NY * yh + yl, 0, :LB] = packed[yh][0][at : at + LB]
                ref[NY * yh + yl, 0, LB:] = packed[yh][1][at : at + HALF]

    for core in range(2):

        @pl.when(place[0] == core)
        def _():
            store(keep, core)
            store(send, 1 - core)


def product(piece, place, atts, blocks):
    count = blocks[0].shape[2] // GROUP
    attn = [pl.BlockSpec(att.shape, lambda z: (0, 0)) for att in atts]
    four = pl.BlockSpec((4, CHUNK, GROUP), lambda z: (0, 0, z))
    pair = pl.BlockSpec((2, CHUNK, GROUP), lambda z: (0, 0, z))
    out = pl.BlockSpec((2 * NY, 1, PACK, 128), lambda z: (0, z, 0, 0))
    shape = jax.ShapeDtypeStruct((2 * NY, count, PACK, 128), jnp.float32)
    flops = 2 * 16 * CHUNK * FEAT * GROUP * count
    return pl.pallas_call(
        functools.partial(product_kernel, piece),
        grid=(count,),
        in_specs=[pl.BlockSpec(memory_space=pltpu.SMEM)]
        + attn
        + [pair, four, four, four, pair],
        out_specs=[out, out],
        out_shape=[shape, shape],
        cost_estimate=pl.CostEstimate(flops=flops, bytes_accessed=8 << 20, transcendentals=0),
        compiler_params=pltpu.CompilerParams(vmem_limit_bytes=32 << 20),
        name="product",
    )(place, *atts, *blocks)


def update_kernel(
    parts,
    weight,
    exp_avg,
    exp_avg_sq,
    left_stats,
    right_stats,
    left_basis,
    right_basis,
    update,
    new_weight,
    moment_out,
    second_out,
    left_new,
    right_new,
):
    def dot(left, right, dims):
        return lax.dot_general(
            left,
            right,
            (dims, ((), ())),
            precision=lax.Precision.HIGHEST,
            preferred_element_type=jnp.float32,
        )

    plain, first, last = ((1,), (0,)), ((0,), (0,)), ((1,), (1,))
    packed = jnp.sum(parts[...], axis=0)
    rest = jnp.concatenate([packed[LB:, : HB - 128], packed[LB:, HB - 128 :]], axis=0)
    gradient = jnp.concatenate([packed[:LB], rest], axis=1)
    left_q, right_q = left_basis[...], right_basis[...]
    moment = beta_one * exp_avg[...] + (1.0 - beta_one) * gradient
    moment_out[...] = moment
    rotated = dot(dot(left_q, gradient, first), right_q, plain)
    second = beta_two * exp_avg_sq[...] + (1.0 - beta_two) * rotated * rotated
    second_out[...] = second
    turned = dot(dot(left_q, moment, first), right_q, plain)
    direction = turned / (jnp.sqrt(second) + epsilon)
    step = dot(dot(left_q, direction, plain), right_q, last)
    update[...] = step
    new_weight[...] = weight[...] * (1.0 - learn_rate * decay_rate) - learn_rate * step
    left_new[...] = beta_two * left_stats[...] + (1.0 - beta_two) * dot(gradient, gradient, last)
    right_new[...] = beta_two * right_stats[...] + (1.0 - beta_two) * dot(gradient, gradient, first)


def local(
    attn_out,
    cotangent,
    gate,
    weight,
    exp_avg,
    exp_avg_sq,
    left_stats,
    right_stats,
    left_basis,
    right_basis,
):
    yh, x, zl, core = (lax.axis_index(name) for name in ("yh", "x", "zl", "c"))
    step = 1 - 2 * core
    sources = [lax.rem(x - step * count + 2 * NX, NX) for count in range(NX)]
    place = jnp.stack([core] + sources + [yh, zl])

    features = attn_out.T
    kept = lax.dynamic_slice_in_dim(features, yh * TOK, TOK, 1)
    away = lax.dynamic_slice_in_dim(features, (1 - yh) * TOK, TOK, 1)
    came = lax.ppermute(away, "yh", SWAP)

    mine_one, mine_two, other_one, other_two = split(place, cotangent)
    pair_one = jnp.stack([mine_one, lax.ppermute(other_one, "zl", SWAP)])
    pair_two = jnp.stack([mine_two, lax.ppermute(other_two, "zl", SWAP)])
    first_one = jnp.concatenate([after(hop(pair_one), came), hop(pair_one, 1)])

    att_own, att_swap = features_of(place, kept, after(came, first_one), gate)
    first_two = jnp.concatenate([after(hop(pair_two), att_own), hop(pair_two, 1)])
    att_beside = lax.ppermute(att_own, "zl", SWAP)
    att_across = lax.ppermute(att_swap, ("zl", "c"), [(0, 3), (1, 2), (2, 1), (3, 0)])
    att_cross = lax.ppermute(after(att_swap, att_beside, att_across), "c", SWAP)
    atts = att_own, att_beside, att_cross, att_across

    second_one = hop(first_one)
    second_two = hop(first_two)
    third_one = hop(after(second_one, first_two))
    third_two = hop(after(second_two, third_one))
    last_one = after(hop(after(third_one, second_two)[:2]), third_two)
    last_two = hop(third_two[:2])
    rings = (
        (pair_one, first_one, second_one, third_one, last_one),
        (pair_two, first_two, second_two, third_two, last_two),
    )

    by_z = []
    for at, blocks in enumerate(rings):
        keep, send = product(at, place, atts, blocks)
        paired = keep + lax.ppermute(send, "c", SWAP)
        by_z.append(jnp.sum(lax.all_to_all(paired, Y, 0, 0), axis=0))
    parts = lax.all_to_all(jnp.concatenate(by_z, axis=0), "zh", 0, 0)

    block = jax.ShapeDtypeStruct((LB, HB), jnp.float32)
    return pl.pallas_call(
        update_kernel,
        out_shape=[block] * 4
        + [
            jax.ShapeDtypeStruct((LB, LB), jnp.float32),
            jax.ShapeDtypeStruct((HB, HB), jnp.float32),
        ],
        name="update",
    )(parts, weight, exp_avg, exp_avg_sq, left_stats, right_stats, left_basis, right_basis)


def solution(mesh):
    axes = ("yh", "x", "zh", "zl", "yl", "c")
    fine = Mesh(mesh.devices.reshape(2, NX, NZH, 2, NY, 2), axes)
    block = P(ROW, COL)
    in_specs = (block, P(COL + ROW, None), P(ROW, None)) + (block,) * 7
    return jax.shard_map(
        local, mesh=fine, in_specs=in_specs, out_specs=(block,) * 6, check_vma=False
    )
```

```python
import functools

import jax
import jax.numpy as jnp
from jax import lax
from jax.experimental import pallas as pl
from jax.experimental.pallas import tpu as pltpu
from jax.sharding import Mesh, PartitionSpec as P

beta_one = 0.9
beta_two = 0.95
epsilon = 1e-08
learn_rate = 0.02
decay_rate = 0.1

D = 3072
LB = 48
HB = 192
NX = 8
NZH = 4
NY = 4
CHUNK = 128
TOK = NX * CHUNK
FEAT = 2 * HB
GROUP = D // 8
HALF = LB // 2
PACK = (LB * HB) // 128
ROW = ("zh", "zl", "yl", "c")
COL = ("yh", "x")
Y = ("yh", "yl")
SWAP = [(0, 1), (1, 0)]


def at_ring(x, zl, c):
    return (x % NX) * 4 + 2 * zl + c


def ring(other_z, other_core):
    pairs = []
    for x in range(NX):
        for zl in range(2):
            for c in range(2):
                to_z, to_c = zl ^ other_z, c ^ other_core
                pairs.append((at_ring(x, zl, c), at_ring(x + 1 - 2 * to_c, to_z, to_c)))
    return pairs


def hop(block, other_z=0, other_core=0):
    return lax.ppermute(block, ("x", "zl", "c"), ring(other_z, other_core))


def after(value, *others):
    return lax.optimization_barrier((value, *others))[0]


def split_kernel(place, cotangent, mine, other):
    for zh in range(NZH):
        for parity, ref in ((place[10], mine), (1 - place[10], other)):
            start = pl.multiple_of((2 * zh + parity) * GROUP, GROUP)
            at = (zh % 2) * GROUP
            ref[zh // 2, :, at : at + GROUP] = cotangent[:, pl.ds(start, GROUP)]


def split(place, cotangent):
    half = jax.ShapeDtypeStruct((2, CHUNK, D // 4), cotangent.dtype)
    return pl.pallas_call(
        split_kernel,
        in_specs=[pl.BlockSpec(memory_space=pltpu.SMEM), pl.BlockSpec((CHUNK, D), lambda: (0, 0))],
        out_shape=[half] * 2,
        name="split",
    )(place, cotangent)


def features_kernel(place, kept, came, gate, out):
    for top, bottom, yh in ((kept, came, 0), (came, kept, 1)):

        @pl.when(place[9] == yh)
        def _():
            out[:HB] = top[...]
            out[HB:FEAT] = bottom[...]

    rest = jnp.concatenate([gate[:, z * GROUP : (z + 1) * GROUP] for z in range(8)], axis=0)
    rows = []
    for _ in range(3):
        part = rest.astype(jnp.bfloat16)
        rest = rest - part.astype(jnp.float32)
        rows.append(part)
    out[FEAT:, :GROUP] = jnp.concatenate(rows + [jnp.zeros_like(rows[0])], axis=0)
    out[FEAT:, GROUP:] = jnp.zeros((32, TOK - GROUP), jnp.bfloat16)


def features_of(place, kept, came, gate):
    def whole(array):
        return pl.BlockSpec(array.shape, lambda: (0, 0))

    return pl.pallas_call(
        features_kernel,
        in_specs=[pl.BlockSpec(memory_space=pltpu.SMEM), whole(kept), whole(came), whole(gate)],
        out_shape=jax.ShapeDtypeStruct((FEAT + 32, TOK), jnp.bfloat16),
        name="features",
    )(place, kept, came, gate)


def product_kernel(
    piece,
    place,
    atts,
    own,
    beside,
    hop_one,
    hop_two,
    hop_three,
    last,
    keep,
    send,
):
    group = 2 * (2 * piece + pl.program_id(0)) + place[10]

    def att(clip, *hops):
        parts = []
        for at in hops:
            columns = pl.ds(pl.multiple_of(place[1 + at] * CHUNK, CHUNK), CHUNK)
            parts.append(atts[clip, :FEAT, columns])
        return parts[0] if len(parts) == 1 else jnp.concatenate(parts, axis=1)

    def dot(left, *blocks):
        right = blocks[0] if len(blocks) == 1 else jnp.concatenate(blocks, axis=0)
        return jnp.dot(left, right, preferred_element_type=jnp.float32)

    total = jnp.zeros((FEAT, GROUP), jnp.float32)
    for which in range(4):
        z = place[10] if which % 2 == 0 else 1 - place[10]
        at = 2 * z + (place[0] if which < 2 else 1 - place[0])
        one, two, three = hop_one[which], hop_two[which], hop_three[which]
        if which < 2:
            near = (own, beside)[which][0]
            clip = dot(att(at, 0, 1), near, one)
            clip += dot(att(at, 2, 3), two, three)
            clip += dot(att(at, 4), last[which])
        else:
            clip = dot(att(at, 1, 2), one, two)
            clip += dot(att(at, 3), three)
        parts = atts[at, FEAT:, :GROUP].astype(jnp.float32)
        rows = lax.broadcasted_iota(jnp.int32, parts.shape, 0)
        mine = (rows & 7 == group) & (rows < 24)
        gate = jnp.sum(jnp.where(mine, parts, 0.0), axis=0, keepdims=True)
        total += gate * clip
    packed = []
    for yh in range(2):
        at = yh * HB
        rest = total[at + 128 : at + HB]
        moved = pltpu.roll(rest, GROUP - HALF, 1)
        packed.append((total[at : at + 128].T, jnp.concatenate([rest, moved], axis=0).T))

    def store(ref, core):
        for yh in range(2):
            for yl in range(NY):
                at = (2 * yl + core) * LB
                ref[NY * yh + yl, 0, :LB] = packed[yh][0][at : at + LB]
                ref[NY * yh + yl, 0, LB:] = packed[yh][1][at : at + HALF]

    for core in range(2):

        @pl.when(place[0] == core)
        def _():
            store(keep, core)
            store(send, 1 - core)


def product(piece, place, atts, own, beside, blocks):
    count = blocks[0].shape[2] // GROUP
    attn = pl.BlockSpec(atts.shape, lambda z: (0, 0, 0))
    near = pl.BlockSpec((1, CHUNK, GROUP), lambda z: (piece, 0, z))
    four = pl.BlockSpec((4, CHUNK, GROUP), lambda z: (0, 0, z))
    pair = pl.BlockSpec((2, CHUNK, GROUP), lambda z: (0, 0, z))
    out = pl.BlockSpec((2 * NY, 1, PACK, 128), lambda z: (0, z, 0, 0))
    shape = jax.ShapeDtypeStruct((2 * NY, count, PACK, 128), jnp.float32)
    flops = 2 * 16 * CHUNK * FEAT * GROUP * count
    return pl.pallas_call(
        functools.partial(product_kernel, piece),
        grid=(count,),
        in_specs=[pl.BlockSpec(memory_space=pltpu.SMEM), attn]
        + [near, near, four, four, four, pair],
        out_specs=[out, out],
        out_shape=[shape, shape],
        cost_estimate=pl.CostEstimate(flops=flops, bytes_accessed=8 << 20, transcendentals=0),
        compiler_params=pltpu.CompilerParams(vmem_limit_bytes=32 << 20),
        name="product",
    )(place, atts, own, beside, *blocks)


def update_kernel(
    parts,
    weight,
    exp_avg,
    exp_avg_sq,
    left_stats,
    right_stats,
    left_basis,
    right_basis,
    update,
    new_weight,
    moment_out,
    second_out,
    left_new,
    right_new,
):
    def dot(left, right, dims):
        return lax.dot_general(
            left,
            right,
            (dims, ((), ())),
            precision=lax.Precision.HIGHEST,
            preferred_element_type=jnp.float32,
        )

    plain, first, last = ((1,), (0,)), ((0,), (0,)), ((1,), (1,))
    packed = jnp.sum(parts[...], axis=0)
    rest = jnp.concatenate([packed[LB:, : HB - 128], packed[LB:, HB - 128 :]], axis=0)
    gradient = jnp.concatenate([packed[:LB], rest], axis=1)
    left_q, right_q = left_basis[...], right_basis[...]
    moment = beta_one * exp_avg[...] + (1.0 - beta_one) * gradient
    moment_out[...] = moment
    rotated = dot(dot(left_q, gradient, first), right_q, plain)
    second = beta_two * exp_avg_sq[...] + (1.0 - beta_two) * rotated * rotated
    second_out[...] = second
    turned = dot(dot(left_q, moment, first), right_q, plain)
    direction = turned / (jnp.sqrt(second) + epsilon)
    step = dot(dot(left_q, direction, plain), right_q, last)
    update[...] = step
    new_weight[...] = weight[...] * (1.0 - learn_rate * decay_rate) - learn_rate * step
    left_new[...] = beta_two * left_stats[...] + (1.0 - beta_two) * dot(gradient, gradient, last)
    right_new[...] = beta_two * right_stats[...] + (1.0 - beta_two) * dot(gradient, gradient, first)


def local(
    attn_out,
    cotangent,
    gate,
    weight,
    exp_avg,
    exp_avg_sq,
    left_stats,
    right_stats,
    left_basis,
    right_basis,
):
    yh, x, zl, core = (lax.axis_index(name) for name in ("yh", "x", "zl", "c"))
    step = 1 - 2 * core
    sources = [lax.rem(x - step * count + 2 * NX, NX) for count in range(NX)]
    place = jnp.stack([core] + sources + [yh, zl])

    features = attn_out.T
    kept = lax.dynamic_slice_in_dim(features, yh * TOK, TOK, 1)
    away = lax.dynamic_slice_in_dim(features, (1 - yh) * TOK, TOK, 1)
    came = lax.ppermute(away, "yh", SWAP)

    mine, other = split(place, cotangent)
    parts = [hop(mine), hop(other, 1, 0), hop(mine, 0, 1), hop(other, 1, 1)]
    swapped = after(came, *parts)
    parts = [after(part, came) for part in parts]
    first_one = jnp.stack([part[0] for part in parts])
    first_two = jnp.stack([part[1] for part in parts])

    att_own = features_of(place, kept, swapped, gate)
    atts = lax.all_gather(att_own, ("zl", "c"))
    beside = lax.ppermute(other, "zl", SWAP)

    second_one = hop(first_one)
    second_two = hop(after(first_two, att_own))
    third_one = hop(after(second_one, first_two))
    third_two = hop(after(second_two, third_one))
    last_one = after(hop(after(third_one, second_two)[:2]), third_two)
    last_two = after(hop(after(third_two, beside)[:2]), last_one)
    rings = (
        (first_one, second_one, third_one, last_one),
        (first_two, second_two, third_two, last_two),
    )

    by_z = []
    for at, blocks in enumerate(rings):
        keep, send = product(at, place, atts, mine, beside, blocks)
        paired = keep + lax.ppermute(send, "c", SWAP)
        by_z.append(jnp.sum(lax.all_to_all(paired, Y, 0, 0), axis=0))
    parts = lax.all_to_all(jnp.concatenate(by_z, axis=0), "zh", 0, 0)

    block = jax.ShapeDtypeStruct((LB, HB), jnp.float32)
    return pl.pallas_call(
        update_kernel,
        out_shape=[block] * 4
        + [
            jax.ShapeDtypeStruct((LB, LB), jnp.float32),
            jax.ShapeDtypeStruct((HB, HB), jnp.float32),
        ],
        name="update",
    )(parts, weight, exp_avg, exp_avg_sq, left_stats, right_stats, left_basis, right_basis)


def solution(mesh):
    axes = ("yh", "x", "zh", "zl", "yl", "c")
    fine = Mesh(mesh.devices.reshape(2, NX, NZH, 2, NY, 2), axes)
    block = P(ROW, COL)
    in_specs = (block, P(COL + ROW, None), P(ROW, None)) + (block,) * 7
    return jax.shard_map(
        local, mesh=fine, in_specs=in_specs, out_specs=(block,) * 6, check_vma=False
    )
```

```python
import functools

import jax
import jax.numpy as jnp
from jax import lax
from jax.experimental import pallas as pl
from jax.experimental.pallas import tpu as pltpu
from jax.sharding import Mesh, PartitionSpec as P

beta_one = 0.9
beta_two = 0.95
epsilon = 1e-08
learn_rate = 0.02
decay_rate = 0.1

D = 3072
LB = 48
HB = 192
NX = 8
NZH = 4
NY = 4
CHUNK = 128
TOK = NX * CHUNK
FEAT = 2 * HB
GROUP = D // 8
HALF = LB // 2
PACK = (LB * HB) // 128
ROW = ("zh", "zl", "yl", "c")
COL = ("yh", "x")
Y = ("yh", "yl")
SWAP = [(0, 1), (1, 0)]


def at_ring(x, zl, c):
    return (x % NX) * 4 + 2 * zl + c


def ring(other_z, other_core):
    pairs = []
    for x in range(NX):
        for zl in range(2):
            for c in range(2):
                to_z, to_c = zl ^ other_z, c ^ other_core
                pairs.append((at_ring(x, zl, c), at_ring(x + 1 - 2 * to_c, to_z, to_c)))
    return pairs


def hop(block, other_z=0, other_core=0):
    return lax.ppermute(block, ("x", "zl", "c"), ring(other_z, other_core))


def after(value, *others):
    return lax.optimization_barrier((value, *others))[0]


def split_kernel(place, cotangent, mine, other):
    for zh in range(NZH):
        for parity, ref in ((place[10], mine), (1 - place[10], other)):
            start = pl.multiple_of((2 * zh + parity) * GROUP, GROUP)
            at = (zh % 2) * GROUP
            ref[zh // 2, :, at : at + GROUP] = cotangent[:, pl.ds(start, GROUP)]


def split(place, cotangent):
    half = jax.ShapeDtypeStruct((2, CHUNK, D // 4), cotangent.dtype)
    return pl.pallas_call(
        split_kernel,
        in_specs=[pl.BlockSpec(memory_space=pltpu.SMEM), pl.BlockSpec((CHUNK, D), lambda: (0, 0))],
        out_shape=[half] * 2,
        name="split",
    )(place, cotangent)


def features_kernel(place, kept, came, gate, out):
    for top, bottom, yh in ((kept, came, 0), (came, kept, 1)):

        @pl.when(place[9] == yh)
        def _():
            for at, hops in enumerate((0, 1, 2, 3, 4, 7, 6, 5)):
                start = pl.multiple_of(place[1 + hops] * CHUNK, CHUNK)
                here = slice(at * CHUNK, (at + 1) * CHUNK)
                out[:HB, here] = top[:, pl.ds(start, CHUNK)]
                out[HB:FEAT, here] = bottom[:, pl.ds(start, CHUNK)]

    rest = jnp.concatenate([gate[:, z * GROUP : (z + 1) * GROUP] for z in range(8)], axis=0)
    rows = []
    for _ in range(3):
        part = rest.astype(jnp.bfloat16)
        rest = rest - part.astype(jnp.float32)
        rows.append(part)
    rows = jnp.concatenate(rows + [jnp.zeros_like(rows[0])], axis=0)
    out[FEAT:, :GROUP] = rows
    out[FEAT:, GROUP : 5 * CHUNK] = jnp.zeros((32, 5 * CHUNK - GROUP), jnp.bfloat16)
    out[FEAT:, 5 * CHUNK :] = rows


def features_of(place, kept, came, gate):
    def whole(array):
        return pl.BlockSpec(array.shape, lambda: (0, 0))

    return pl.pallas_call(
        features_kernel,
        in_specs=[pl.BlockSpec(memory_space=pltpu.SMEM), whole(kept), whole(came), whole(gate)],
        out_shape=jax.ShapeDtypeStruct((FEAT + 32, TOK), jnp.bfloat16),
        name="features",
    )(place, kept, came, gate)


def product_kernel(
    piece,
    place,
    att_own,
    att_beside,
    att_cross,
    own,
    beside,
    hop_one,
    hop_two,
    hop_three,
    last,
    keep,
    send,
):
    group = 2 * (2 * piece + pl.program_id(0)) + place[10]

    def dot(left, *blocks):
        right = blocks[0] if len(blocks) == 1 else jnp.concatenate(blocks, axis=0)
        return jnp.dot(left, right, preferred_element_type=jnp.float32)

    total = jnp.zeros((FEAT, GROUP), jnp.float32)
    for which, att in enumerate((att_own, att_beside, att_cross.at[0], att_cross.at[1])):
        one, two, three = hop_one[which], hop_two[which], hop_three[which]
        if which < 2:
            near = (own, beside)[which][0]
            clip = dot(att[:FEAT, : 2 * CHUNK], near, one)
            clip += dot(att[:FEAT, 2 * CHUNK : 4 * CHUNK], two, three)
            clip += dot(att[:FEAT, 4 * CHUNK : 5 * CHUNK], last[which])
        else:
            clip = dot(att[:FEAT, : 2 * CHUNK], one, two)
            clip += dot(att[:FEAT, 2 * CHUNK :], three)
        parts = att[FEAT:, :GROUP].astype(jnp.float32)
        rows = lax.broadcasted_iota(jnp.int32, parts.shape, 0)
        mine = (rows & 7 == group) & (rows < 24)
        gate = jnp.sum(jnp.where(mine, parts, 0.0), axis=0, keepdims=True)
        total += gate * clip
    packed = []
    for yh in range(2):
        at = yh * HB
        rest = total[at + 128 : at + HB]
        moved = pltpu.roll(rest, GROUP - HALF, 1)
        packed.append((total[at : at + 128].T, jnp.concatenate([rest, moved], axis=0).T))

    def store(ref, core):
        for yh in range(2):
            for yl in range(NY):
                at = (2 * yl + core) * LB
                ref[NY * yh + yl, 0, :LB] = packed[yh][0][at : at + LB]
                ref[NY * yh + yl, 0, LB:] = packed[yh][1][at : at + HALF]

    for core in range(2):

        @pl.when(place[0] == core)
        def _():
            store(keep, core)
            store(send, 1 - core)


def product(piece, place, atts, own, beside, blocks):
    count = blocks[0].shape[2] // GROUP
    attn = [pl.BlockSpec(att.shape, lambda z, rank=att.ndim: (0,) * rank) for att in atts]
    near = pl.BlockSpec((1, CHUNK, GROUP), lambda z: (piece, 0, z))
    four = pl.BlockSpec((4, CHUNK, GROUP), lambda z: (0, 0, z))
    pair = pl.BlockSpec((2, CHUNK, GROUP), lambda z: (0, 0, z))
    out = pl.BlockSpec((2 * NY, 1, PACK, 128), lambda z: (0, z, 0, 0))
    shape = jax.ShapeDtypeStruct((2 * NY, count, PACK, 128), jnp.float32)
    flops = 2 * 16 * CHUNK * FEAT * GROUP * count
    return pl.pallas_call(
        functools.partial(product_kernel, piece),
        grid=(count,),
        in_specs=[pl.BlockSpec(memory_space=pltpu.SMEM)]
        + attn
        + [near, near, four, four, four, pair],
        out_specs=[out, out],
        out_shape=[shape, shape],
        cost_estimate=pl.CostEstimate(flops=flops, bytes_accessed=8 << 20, transcendentals=0),
        compiler_params=pltpu.CompilerParams(vmem_limit_bytes=32 << 20),
        name="product",
    )(place, *atts, own, beside, *blocks)


def update_kernel(
    parts,
    weight,
    exp_avg,
    exp_avg_sq,
    left_stats,
    right_stats,
    left_basis,
    right_basis,
    update,
    new_weight,
    moment_out,
    second_out,
    left_new,
    right_new,
):
    def dot(left, right, dims):
        return lax.dot_general(
            left,
            right,
            (dims, ((), ())),
            precision=lax.Precision.HIGHEST,
            preferred_element_type=jnp.float32,
        )

    plain, first, last = ((1,), (0,)), ((0,), (0,)), ((1,), (1,))
    packed = jnp.sum(parts[...], axis=0)
    rest = jnp.concatenate([packed[LB:, : HB - 128], packed[LB:, HB - 128 :]], axis=0)
    gradient = jnp.concatenate([packed[:LB], rest], axis=1)
    left_q, right_q = left_basis[...], right_basis[...]
    moment = beta_one * exp_avg[...] + (1.0 - beta_one) * gradient
    moment_out[...] = moment
    rotated = dot(dot(left_q, gradient, first), right_q, plain)
    second = beta_two * exp_avg_sq[...] + (1.0 - beta_two) * rotated * rotated
    second_out[...] = second
    turned = dot(dot(left_q, moment, first), right_q, plain)
    direction = turned / (jnp.sqrt(second) + epsilon)
    step = dot(dot(left_q, direction, plain), right_q, last)
    update[...] = step
    new_weight[...] = weight[...] * (1.0 - learn_rate * decay_rate) - learn_rate * step
    left_new[...] = beta_two * left_stats[...] + (1.0 - beta_two) * dot(gradient, gradient, last)
    right_new[...] = beta_two * right_stats[...] + (1.0 - beta_two) * dot(gradient, gradient, first)


def local(
    attn_out,
    cotangent,
    gate,
    weight,
    exp_avg,
    exp_avg_sq,
    left_stats,
    right_stats,
    left_basis,
    right_basis,
):
    yh, x, zl, core = (lax.axis_index(name) for name in ("yh", "x", "zl", "c"))
    step = 1 - 2 * core
    sources = [lax.rem(x - step * count + 2 * NX, NX) for count in range(NX)]
    place = jnp.stack([core] + sources + [yh, zl])

    features = attn_out.T
    kept = lax.dynamic_slice_in_dim(features, yh * TOK, TOK, 1)
    away = lax.dynamic_slice_in_dim(features, (1 - yh) * TOK, TOK, 1)
    came = lax.ppermute(away, "yh", SWAP)

    mine, other = split(place, cotangent)
    parts = [hop(mine), hop(other, 1, 0), hop(mine, 0, 1), hop(other, 1, 1)]
    beside = lax.ppermute(other, "zl", SWAP)
    parts = [after(part, came, beside) for part in parts]
    first_one = jnp.stack([part[0] for part in parts])
    first_two = jnp.stack([part[1] for part in parts])

    att_own = features_of(place, kept, after(came, first_two), gate)
    att_beside = lax.ppermute(att_own, "zl", SWAP)
    crossing = jnp.stack([att_own[:, 5 * CHUNK :], att_beside[:, 5 * CHUNK :]])
    att_cross = lax.ppermute(crossing, "c", SWAP)
    atts = att_own, att_beside, att_cross

    second_one = hop(first_one)
    second_two = hop(first_two)
    third_one = hop(after(second_one, first_two))
    third_two = hop(after(second_two, first_one))
    last_one = after(hop(after(third_one, second_two)[:2]), third_two)
    last_two = after(hop(after(third_two, second_one)[:2]), third_one)
    rings = (
        (first_one, second_one, third_one, last_one),
        (first_two, second_two, third_two, last_two),
    )

    by_z = []
    for at, blocks in enumerate(rings):
        keep, send = product(at, place, atts, mine, beside, blocks)
        paired = keep + lax.ppermute(send, "c", SWAP)
        by_z.append(jnp.sum(lax.all_to_all(paired, Y, 0, 0), axis=0))
    parts = lax.all_to_all(jnp.concatenate(by_z, axis=0), "zh", 0, 0)

    block = jax.ShapeDtypeStruct((LB, HB), jnp.float32)
    return pl.pallas_call(
        update_kernel,
        out_shape=[block] * 4
        + [
            jax.ShapeDtypeStruct((LB, LB), jnp.float32),
            jax.ShapeDtypeStruct((HB, HB), jnp.float32),
        ],
        name="update",
    )(parts, weight, exp_avg, exp_avg_sq, left_stats, right_stats, left_basis, right_basis)


def solution(mesh):
    axes = ("yh", "x", "zh", "zl", "yl", "c")
    fine = Mesh(mesh.devices.reshape(2, NX, NZH, 2, NY, 2), axes)
    block = P(ROW, COL)
    in_specs = (block, P(COL + ROW, None), P(ROW, None)) + (block,) * 7
    return jax.shard_map(
        local, mesh=fine, in_specs=in_specs, out_specs=(block,) * 6, check_vma=False
    )
```

```python
import functools

import jax
import jax.numpy as jnp
from jax import lax
from jax.experimental import pallas as pl
from jax.experimental.pallas import tpu as pltpu
from jax.sharding import Mesh, PartitionSpec as P

beta_one = 0.9
beta_two = 0.95
epsilon = 1e-08
learn_rate = 0.02
decay_rate = 0.1

D = 3072
LB = 48
HB = 192
NX = 8
NZH = 4
NY = 4
CHUNK = 128
TOK = NX * CHUNK
FEAT = 2 * HB
GROUP = D // 8
HALF = LB // 2
PACK = (LB * HB) // 128
ROW = ("zh", "zl", "yl", "c")
COL = ("yh", "x")
Y = ("yh", "yl")
SWAP = [(0, 1), (1, 0)]


def at_ring(x, zl, c):
    return (x % NX) * 4 + 2 * zl + c


def ring(other_z, other_core):
    pairs = []
    for x in range(NX):
        for zl in range(2):
            for c in range(2):
                to_z, to_c = zl ^ other_z, c ^ other_core
                pairs.append((at_ring(x, zl, c), at_ring(x + 1 - 2 * to_c, to_z, to_c)))
    return pairs


def hop(block, other_z=0, other_core=0):
    return lax.ppermute(block, ("x", "zl", "c"), ring(other_z, other_core))


def after(value, *others):
    return lax.optimization_barrier((value, *others))[0]


def split_kernel(place, cotangent, mine, other):
    for zh in range(NZH):
        for parity, ref in ((place[10], mine), (1 - place[10], other)):
            start = pl.multiple_of((2 * zh + parity) * GROUP, GROUP)
            at = (zh % 2) * GROUP
            ref[zh // 2, :, at : at + GROUP] = cotangent[:, pl.ds(start, GROUP)]


def split(place, cotangent):
    half = jax.ShapeDtypeStruct((2, CHUNK, D // 4), cotangent.dtype)
    return pl.pallas_call(
        split_kernel,
        in_specs=[pl.BlockSpec(memory_space=pltpu.SMEM), pl.BlockSpec((CHUNK, D), lambda: (0, 0))],
        out_shape=[half] * 2,
        name="split",
    )(place, cotangent)


def features_kernel(place, kept, came, gate, out):
    for top, bottom, yh in ((kept, came, 0), (came, kept, 1)):

        @pl.when(place[9] == yh)
        def _():
            for at, hops in enumerate((0, 1, 2, 3, 4, 7, 6, 5)):
                start = pl.multiple_of(place[1 + hops] * CHUNK, CHUNK)
                here = slice(at * CHUNK, (at + 1) * CHUNK)
                out[:HB, here] = top[:, pl.ds(start, CHUNK)]
                out[HB:FEAT, here] = bottom[:, pl.ds(start, CHUNK)]

    rest = jnp.concatenate([gate[:, z * GROUP : (z + 1) * GROUP] for z in range(8)], axis=0)
    rows = []
    for _ in range(3):
        part = rest.astype(jnp.bfloat16)
        rest = rest - part.astype(jnp.float32)
        rows.append(part)
    rows = jnp.concatenate(rows + [jnp.zeros_like(rows[0])], axis=0)
    out[FEAT:, :GROUP] = rows
    out[FEAT:, GROUP : 5 * CHUNK] = jnp.zeros((32, 5 * CHUNK - GROUP), jnp.bfloat16)
    out[FEAT:, 5 * CHUNK :] = rows


def features_of(place, kept, came, gate):
    def whole(array):
        return pl.BlockSpec(array.shape, lambda: (0, 0))

    return pl.pallas_call(
        features_kernel,
        in_specs=[pl.BlockSpec(memory_space=pltpu.SMEM), whole(kept), whole(came), whole(gate)],
        out_shape=jax.ShapeDtypeStruct((FEAT + 32, TOK), jnp.bfloat16),
        name="features",
    )(place, kept, came, gate)


def product_kernel(
    piece,
    place,
    att_own,
    att_beside,
    att_cross,
    own,
    beside,
    hop_one,
    hop_two,
    hop_three,
    last,
    keep,
    send,
):
    group = 2 * (2 * piece + pl.program_id(0)) + place[10]

    def dot(left, *blocks):
        right = blocks[0] if len(blocks) == 1 else jnp.concatenate(blocks, axis=0)
        return jnp.dot(left, right, preferred_element_type=jnp.float32)

    total = jnp.zeros((FEAT, GROUP), jnp.float32)
    for which, att in enumerate((att_own, att_beside, att_cross.at[0], att_cross.at[1])):
        one, two, three = hop_one[which], hop_two[which], hop_three[which]
        if which < 2:
            near = (own, beside)[which][0]
            clip = dot(att[:FEAT, : 2 * CHUNK], near, one)
            clip += dot(att[:FEAT, 2 * CHUNK : 4 * CHUNK], two, three)
            clip += dot(att[:FEAT, 4 * CHUNK : 5 * CHUNK], last[which])
        else:
            clip = dot(att[:FEAT, : 2 * CHUNK], one, two)
            clip += dot(att[:FEAT, 2 * CHUNK :], three)
        parts = att[FEAT:, :GROUP].astype(jnp.float32)
        rows = lax.broadcasted_iota(jnp.int32, parts.shape, 0)
        mine = (rows & 7 == group) & (rows < 24)
        gate = jnp.sum(jnp.where(mine, parts, 0.0), axis=0, keepdims=True)
        total += gate * clip
    packed = []
    for yh in range(2):
        at = yh * HB
        rest = total[at + 128 : at + HB]
        moved = pltpu.roll(rest, GROUP - HALF, 1)
        packed.append((total[at : at + 128].T, jnp.concatenate([rest, moved], axis=0).T))

    def store(ref, core):
        for yh in range(2):
            for yl in range(NY):
                at = (2 * yl + core) * LB
                ref[NY * yh + yl, 0, :LB] = packed[yh][0][at : at + LB]
                ref[NY * yh + yl, 0, LB:] = packed[yh][1][at : at + HALF]

    for core in range(2):

        @pl.when(place[0] == core)
        def _():
            store(keep, core)
            store(send, 1 - core)


def product(piece, place, atts, own, beside, blocks):
    count = blocks[0].shape[2] // GROUP
    attn = [pl.BlockSpec(att.shape, lambda z, rank=att.ndim: (0,) * rank) for att in atts]
    near = pl.BlockSpec((1, CHUNK, GROUP), lambda z: (piece, 0, z))
    four = pl.BlockSpec((4, CHUNK, GROUP), lambda z: (0, 0, z))
    pair = pl.BlockSpec((2, CHUNK, GROUP), lambda z: (0, 0, z))
    out = pl.BlockSpec((2 * NY, 1, PACK, 128), lambda z: (0, z, 0, 0))
    shape = jax.ShapeDtypeStruct((2 * NY, count, PACK, 128), jnp.float32)
    flops = 2 * 16 * CHUNK * FEAT * GROUP * count
    return pl.pallas_call(
        functools.partial(product_kernel, piece),
        grid=(count,),
        in_specs=[pl.BlockSpec(memory_space=pltpu.SMEM)]
        + attn
        + [near, near, four, four, four, pair],
        out_specs=[out, out],
        out_shape=[shape, shape],
        cost_estimate=pl.CostEstimate(flops=flops, bytes_accessed=8 << 20, transcendentals=0),
        compiler_params=pltpu.CompilerParams(vmem_limit_bytes=16 << 20),
        name="product",
    )(place, *atts, own, beside, *blocks)


def update_kernel(
    parts,
    weight,
    exp_avg,
    exp_avg_sq,
    left_stats,
    right_stats,
    left_basis,
    right_basis,
    update,
    new_weight,
    moment_out,
    second_out,
    left_new,
    right_new,
):
    def dot(left, right, dims):
        return lax.dot_general(
            left,
            right,
            (dims, ((), ())),
            precision=lax.Precision.HIGHEST,
            preferred_element_type=jnp.float32,
        )

    plain, first, last = ((1,), (0,)), ((0,), (0,)), ((1,), (1,))
    packed = jnp.sum(parts[...], axis=0)
    rest = jnp.concatenate([packed[LB:, : HB - 128], packed[LB:, HB - 128 :]], axis=0)
    gradient = jnp.concatenate([packed[:LB], rest], axis=1)
    left_q, right_q = left_basis[...], right_basis[...]
    moment = beta_one * exp_avg[...] + (1.0 - beta_one) * gradient
    moment_out[...] = moment
    rotated = dot(dot(left_q, gradient, first), right_q, plain)
    second = beta_two * exp_avg_sq[...] + (1.0 - beta_two) * rotated * rotated
    second_out[...] = second
    turned = dot(dot(left_q, moment, first), right_q, plain)
    direction = turned / (jnp.sqrt(second) + epsilon)
    step = dot(dot(left_q, direction, plain), right_q, last)
    update[...] = step
    new_weight[...] = weight[...] * (1.0 - learn_rate * decay_rate) - learn_rate * step
    left_new[...] = beta_two * left_stats[...] + (1.0 - beta_two) * dot(gradient, gradient, last)
    right_new[...] = beta_two * right_stats[...] + (1.0 - beta_two) * dot(gradient, gradient, first)


def local(
    attn_out,
    cotangent,
    gate,
    weight,
    exp_avg,
    exp_avg_sq,
    left_stats,
    right_stats,
    left_basis,
    right_basis,
):
    yh, x, zl, core = (lax.axis_index(name) for name in ("yh", "x", "zl", "c"))
    step = 1 - 2 * core
    sources = [lax.rem(x - step * count + 2 * NX, NX) for count in range(NX)]
    place = jnp.stack([core] + sources + [yh, zl])

    features = attn_out.T
    kept = lax.dynamic_slice_in_dim(features, yh * TOK, TOK, 1)
    away = lax.dynamic_slice_in_dim(features, (1 - yh) * TOK, TOK, 1)
    came = lax.ppermute(away, "yh", SWAP)

    mine, other = split(place, cotangent)
    parts = [hop(mine), hop(other, 1, 0), hop(mine, 0, 1), hop(other, 1, 1)]
    beside = lax.ppermute(other, "zl", SWAP)
    parts = [after(part, came) for part in parts]
    first_one = jnp.stack([part[0] for part in parts])
    first_two = jnp.stack([part[1] for part in parts])

    att_own = features_of(place, kept, after(came, first_two), gate)
    att_beside = lax.ppermute(att_own, "zl", SWAP)
    crossing = jnp.stack([att_own[:, 5 * CHUNK :], att_beside[:, 5 * CHUNK :]])
    att_cross = lax.ppermute(after(crossing, beside), "c", SWAP)
    atts = att_own, att_beside, att_cross

    second_one = hop(first_one)
    second_two = hop(first_two)
    third_one = hop(after(second_one, first_two))
    third_two = hop(after(second_two, first_one))
    last_one = after(hop(after(third_one, second_two)[:2]), third_two)
    last_two = after(hop(after(third_two, second_one)[:2]), third_one)
    rings = (
        (first_one, second_one, third_one, last_one),
        (first_two, second_two, third_two, last_two),
    )

    by_z = []
    for at, blocks in enumerate(rings):
        keep, send = product(at, place, atts, mine, beside, blocks)
        paired = keep + lax.ppermute(send, "c", SWAP)
        by_z.append(jnp.sum(lax.all_to_all(paired, Y, 0, 0), axis=0))
    parts = lax.all_to_all(jnp.concatenate(by_z, axis=0), "zh", 0, 0)

    block = jax.ShapeDtypeStruct((LB, HB), jnp.float32)
    return pl.pallas_call(
        update_kernel,
        out_shape=[block] * 4
        + [
            jax.ShapeDtypeStruct((LB, LB), jnp.float32),
            jax.ShapeDtypeStruct((HB, HB), jnp.float32),
        ],
        name="update",
    )(parts, weight, exp_avg, exp_avg_sq, left_stats, right_stats, left_basis, right_basis)


def solution(mesh):
    axes = ("yh", "x", "zh", "zl", "yl", "c")
    fine = Mesh(mesh.devices.reshape(2, NX, NZH, 2, NY, 2), axes)
    block = P(ROW, COL)
    in_specs = (block, P(COL + ROW, None), P(ROW, None)) + (block,) * 7
    return jax.shard_map(
        local, mesh=fine, in_specs=in_specs, out_specs=(block,) * 6, check_vma=False
    )
```

```python
import functools

import jax
import jax.numpy as jnp
from jax import lax
from jax.experimental import pallas as pl
from jax.experimental.pallas import tpu as pltpu
from jax.sharding import Mesh, PartitionSpec as P

beta_one = 0.9
beta_two = 0.95
epsilon = 1e-08
learn_rate = 0.02
decay_rate = 0.1

D = 3072
LB = 48
HB = 192
NX = 8
NZH = 4
NY = 4
CHUNK = 128
TOK = NX * CHUNK
FEAT = 2 * HB
GROUP = D // 8
HALF = LB // 2
PACK = (LB * HB) // 128
ROW = ("zh", "zl", "yl", "c")
COL = ("yh", "x")
Y = ("yh", "yl")
SWAP = [(0, 1), (1, 0)]


def at_ring(x, zl, c):
    return (x % NX) * 4 + 2 * zl + c


def ring(other_z, other_core):
    pairs = []
    for x in range(NX):
        for zl in range(2):
            for c in range(2):
                to_z, to_c = zl ^ other_z, c ^ other_core
                pairs.append((at_ring(x, zl, c), at_ring(x + 1 - 2 * to_c, to_z, to_c)))
    return pairs


def hop(block, other_z=0, other_core=0):
    return lax.ppermute(block, ("x", "zl", "c"), ring(other_z, other_core))


def after(value, *others):
    return lax.optimization_barrier((value, *others))[0]


def split_kernel(place, cotangent, mine, other):
    for zh in range(NZH):
        for parity, ref in ((place[10], mine), (1 - place[10], other)):
            start = pl.multiple_of((2 * zh + parity) * GROUP, GROUP)
            at = (zh % 2) * GROUP
            ref[zh // 2, :, at : at + GROUP] = cotangent[:, pl.ds(start, GROUP)]


def split(place, cotangent):
    half = jax.ShapeDtypeStruct((2, CHUNK, D // 4), cotangent.dtype)
    return pl.pallas_call(
        split_kernel,
        in_specs=[pl.BlockSpec(memory_space=pltpu.SMEM), pl.BlockSpec((CHUNK, D), lambda: (0, 0))],
        out_shape=[half] * 2,
        name="split",
    )(place, cotangent)


def features_kernel(place, kept, came, gate, out):
    for top, bottom, yh in ((kept, came, 0), (came, kept, 1)):

        @pl.when(place[9] == yh)
        def _():
            for at, hops in enumerate((0, 1, 2, 3, 4, 7, 6, 5)):
                start = pl.multiple_of(place[1 + hops] * CHUNK, CHUNK)
                here = slice(at * CHUNK, (at + 1) * CHUNK)
                out[:HB, here] = top[:, pl.ds(start, CHUNK)]
                out[HB:FEAT, here] = bottom[:, pl.ds(start, CHUNK)]

    rest = jnp.concatenate([gate[:, z * GROUP : (z + 1) * GROUP] for z in range(8)], axis=0)
    rows = []
    for _ in range(3):
        part = rest.astype(jnp.bfloat16)
        rest = rest - part.astype(jnp.float32)
        rows.append(part)
    rows = jnp.concatenate(rows + [jnp.zeros_like(rows[0])], axis=0)
    out[FEAT:, :GROUP] = rows
    out[FEAT:, GROUP : 5 * CHUNK] = jnp.zeros((32, 5 * CHUNK - GROUP), jnp.bfloat16)
    out[FEAT:, 5 * CHUNK :] = rows


def features_of(place, kept, came, gate):
    def whole(array):
        return pl.BlockSpec(array.shape, lambda: (0, 0))

    return pl.pallas_call(
        features_kernel,
        in_specs=[pl.BlockSpec(memory_space=pltpu.SMEM), whole(kept), whole(came), whole(gate)],
        out_shape=jax.ShapeDtypeStruct((FEAT + 32, TOK), jnp.bfloat16),
        name="features",
    )(place, kept, came, gate)


def product_kernel(
    piece,
    place,
    att_own,
    att_beside,
    att_cross,
    own,
    beside,
    hop_one,
    hop_two,
    hop_three,
    last,
    keep,
    send,
):
    group = 2 * (2 * piece + pl.program_id(0)) + place[10]

    def dot(left, *blocks):
        right = blocks[0] if len(blocks) == 1 else jnp.concatenate(blocks, axis=0)
        return jnp.dot(left, right, preferred_element_type=jnp.float32)

    total = jnp.zeros((FEAT, GROUP), jnp.float32)
    for which, att in enumerate((att_own, att_beside, att_cross.at[0], att_cross.at[1])):
        one, two, three = hop_one[which], hop_two[which], hop_three[which]
        if which < 2:
            near = (own, beside)[which][0]
            clip = dot(att[:FEAT, : 2 * CHUNK], near, one)
            clip += dot(att[:FEAT, 2 * CHUNK : 4 * CHUNK], two, three)
            clip += dot(att[:FEAT, 4 * CHUNK : 5 * CHUNK], last[which])
        else:
            clip = dot(att[:FEAT, : 2 * CHUNK], one, two)
            clip += dot(att[:FEAT, 2 * CHUNK :], three)
        parts = att[FEAT:, :GROUP].astype(jnp.float32)
        rows = lax.broadcasted_iota(jnp.int32, parts.shape, 0)
        mine = (rows & 7 == group) & (rows < 24)
        gate = jnp.sum(jnp.where(mine, parts, 0.0), axis=0, keepdims=True)
        total += gate * clip
    packed = []
    for yh in range(2):
        at = yh * HB
        rest = total[at + 128 : at + HB]
        moved = pltpu.roll(rest, GROUP - HALF, 1)
        packed.append((total[at : at + 128].T, jnp.concatenate([rest, moved], axis=0).T))

    def store(ref, core):
        for yh in range(2):
            for yl in range(NY):
                at = (2 * yl + core) * LB
                ref[NY * yh + yl, 0, :LB] = packed[yh][0][at : at + LB]
                ref[NY * yh + yl, 0, LB:] = packed[yh][1][at : at + HALF]

    for core in range(2):

        @pl.when(place[0] == core)
        def _():
            store(keep, core)
            store(send, 1 - core)


def product(piece, place, atts, own, beside, blocks):
    count = blocks[0].shape[2] // GROUP
    attn = [pl.BlockSpec(att.shape, lambda z, rank=att.ndim: (0,) * rank) for att in atts]
    near = pl.BlockSpec((1, CHUNK, GROUP), lambda z: (piece, 0, z))
    four = pl.BlockSpec((4, CHUNK, GROUP), lambda z: (0, 0, z))
    pair = pl.BlockSpec((2, CHUNK, GROUP), lambda z: (0, 0, z))
    out = pl.BlockSpec((2 * NY, 1, PACK, 128), lambda z: (0, z, 0, 0))
    shape = jax.ShapeDtypeStruct((2 * NY, count, PACK, 128), jnp.float32)
    flops = 2 * 16 * CHUNK * FEAT * GROUP * count
    return pl.pallas_call(
        functools.partial(product_kernel, piece),
        grid=(count,),
        in_specs=[pl.BlockSpec(memory_space=pltpu.SMEM)]
        + attn
        + [near, near, four, four, four, pair],
        out_specs=[out, out],
        out_shape=[shape, shape],
        cost_estimate=pl.CostEstimate(flops=flops, bytes_accessed=8 << 20, transcendentals=0),
        compiler_params=pltpu.CompilerParams(vmem_limit_bytes=16 << 20),
        name="product",
    )(place, *atts, own, beside, *blocks)


def update_kernel(
    parts,
    weight,
    exp_avg,
    exp_avg_sq,
    left_stats,
    right_stats,
    left_basis,
    right_basis,
    update,
    new_weight,
    moment_out,
    second_out,
    left_new,
    right_new,
):
    def dot(left, right, dims):
        return lax.dot_general(
            left,
            right,
            (dims, ((), ())),
            precision=lax.Precision.HIGHEST,
            preferred_element_type=jnp.float32,
        )

    plain, first, last = ((1,), (0,)), ((0,), (0,)), ((1,), (1,))
    packed = jnp.sum(parts[...], axis=0)
    rest = jnp.concatenate([packed[LB:, : HB - 128], packed[LB:, HB - 128 :]], axis=0)
    gradient = jnp.concatenate([packed[:LB], rest], axis=1)
    left_q, right_q = left_basis[...], right_basis[...]
    moment = beta_one * exp_avg[...] + (1.0 - beta_one) * gradient
    moment_out[...] = moment
    rotated = dot(dot(left_q, gradient, first), right_q, plain)
    second = beta_two * exp_avg_sq[...] + (1.0 - beta_two) * rotated * rotated
    second_out[...] = second
    turned = dot(dot(left_q, moment, first), right_q, plain)
    direction = turned / (jnp.sqrt(second) + epsilon)
    step = dot(dot(left_q, direction, plain), right_q, last)
    update[...] = step
    new_weight[...] = weight[...] * (1.0 - learn_rate * decay_rate) - learn_rate * step
    left_new[...] = beta_two * left_stats[...] + (1.0 - beta_two) * dot(gradient, gradient, last)
    right_new[...] = beta_two * right_stats[...] + (1.0 - beta_two) * dot(gradient, gradient, first)


def local(
    attn_out,
    cotangent,
    gate,
    weight,
    exp_avg,
    exp_avg_sq,
    left_stats,
    right_stats,
    left_basis,
    right_basis,
):
    yh, x, zl, core = (lax.axis_index(name) for name in ("yh", "x", "zl", "c"))
    step = 1 - 2 * core
    sources = [lax.rem(x - step * count + 2 * NX, NX) for count in range(NX)]
    place = jnp.stack([core] + sources + [yh, zl])

    features = attn_out.T
    kept = lax.dynamic_slice_in_dim(features, yh * TOK, TOK, 1)
    away = lax.dynamic_slice_in_dim(features, (1 - yh) * TOK, TOK, 1)
    came = lax.ppermute(away, "yh", SWAP)

    mine, other = split(place, cotangent)
    beside = lax.ppermute(other, "zl", SWAP)
    pair = jnp.stack([mine, beside], axis=1)
    parts = [hop(pair), hop(pair, other_core=1)]
    first_one = jnp.concatenate([part[0] for part in parts])
    first_two = jnp.concatenate([part[1] for part in parts])

    att_own = features_of(place, kept, after(came, first_one), gate)
    att_beside = lax.ppermute(att_own, "zl", SWAP)
    crossing = jnp.stack([att_own[:, 5 * CHUNK :], att_beside[:, 5 * CHUNK :]])
    att_cross = lax.ppermute(crossing, "c", SWAP)
    atts = att_own, att_beside, att_cross

    second_one = hop(first_one)
    second_two = hop(first_two)
    third_one = hop(after(second_one, first_two, att_own))
    third_two = hop(after(second_two, first_one))
    last_one = after(hop(after(third_one, second_two)[:2]), third_two)
    last_two = after(hop(after(third_two, second_one)[:2]), third_one)
    rings = (
        (first_one, second_one, third_one, last_one),
        (first_two, second_two, third_two, last_two),
    )

    by_z = []
    for at, blocks in enumerate(rings):
        keep, send = product(at, place, atts, mine, beside, blocks)
        paired = keep + lax.ppermute(send, "c", SWAP)
        by_z.append(jnp.sum(lax.all_to_all(paired, Y, 0, 0), axis=0))
    parts = lax.all_to_all(jnp.concatenate(by_z, axis=0), "zh", 0, 0)

    block = jax.ShapeDtypeStruct((LB, HB), jnp.float32)
    return pl.pallas_call(
        update_kernel,
        out_shape=[block] * 4
        + [
            jax.ShapeDtypeStruct((LB, LB), jnp.float32),
            jax.ShapeDtypeStruct((HB, HB), jnp.float32),
        ],
        name="update",
    )(parts, weight, exp_avg, exp_avg_sq, left_stats, right_stats, left_basis, right_basis)


def solution(mesh):
    axes = ("yh", "x", "zh", "zl", "yl", "c")
    fine = Mesh(mesh.devices.reshape(2, NX, NZH, 2, NY, 2), axes)
    block = P(ROW, COL)
    in_specs = (block, P(COL + ROW, None), P(ROW, None)) + (block,) * 7
    return jax.shard_map(
        local, mesh=fine, in_specs=in_specs, out_specs=(block,) * 6, check_vma=False
    )
```
